256 devices in a mesh: dp: 4 (over z_lo, core), expert: 64 (over x, y, z_hi).
Axes of the slice: x: 4, y: 4, z: 8 (z_hi: 4, z_lo: 2; z = z_hi * 2 + z_lo), core: 2. Of those that a mesh axis runs over, the one named last changes fastest.
Arguments:
- tokens: bfloat16 [32768, 2048], P(('dp', 'expert')), may hold values from -6 to 6
- d_out: bfloat16 [32768, 2048], P(('dp', 'expert')), may hold values from -6 to 6
- route_probs: bfloat16 [32768, 8], P(('dp', 'expert')), may hold values from 0.019897461 to 0.3984375
- routes: int32 [32768, 8], P(('dp', 'expert')), may hold values from 0 to 63, all different within a row; in each aligned block of 128 rows (0 to 127, 128 to 255, ...) at most 17 rows name the same one
- w_gate: bfloat16 [64, 2048, 512], P('expert'), may hold values from -0.125 to 0.125
- w_up: bfloat16 [64, 2048, 512], P('expert'), may hold values from -0.125 to 0.125
- w_down: bfloat16 [64, 512, 2048], P('expert'), may hold values from -0.25 to 0.25
Outputs:
- d_tokens: bfloat16 [32768, 2048], P(('dp', 'expert'))
- d_probs: bfloat16 [32768, 8], P(('dp', 'expert'))
- grad_gate: bfloat16 [64, 2048, 512], P('expert', 'dp')
- grad_up: bfloat16 [64, 2048, 512], P('expert', 'dp')
- grad_down: bfloat16 [64, 512, 2048], P('expert', None, 'dp')
The draws below stay inside these ranges and needn't reach their ends.
Inputs may be any that keep to these rules, and one draw needn't show every extreme that they name: `routes`: each row names 8 different experts. In the rows of one device each expert is named by at most 17 rows, a bound that some block reaches.
All inputs are finite; a program needn't handle non-finite values.
Results may differ from the reference program's by a relative error of at most 0.013.
Values may be sent and summed in bfloat16 or wider, within the bound.
A program may use at most 128 MiB of HBM per device.

```python
import math
import jax
import jax.numpy as jnp
import numpy as np
from jax import lax

D = 2048
FFW = 512
TOP = 8
TOK_DEV = 128
EXPERTS = 64
CAP = 17
TOKENS = 32768
N_DP = 4
N_EXPERT = 64


def level_of(key, dims, pieces, smallest, largest):
    factor_of, own = 1.0, jax.random.fold_in(key, 6)
    for dim, shards_of in pieces:
        draws = jnp.exp(jax.random.uniform(jax.random.fold_in(own, dim), (shards_of,), jnp.float32, smallest / len(pieces), largest / len(pieces)))
        factor_of = factor_of * jnp.repeat(draws, dims[dim] // shards_of).reshape([-1 if axis == dim else 1 for axis in range(len(dims))])
    return factor_of


def deal_out(key, own, number, rows, number_of, top, bound, slope):
    ranking = jax.random.permutation(key, number_of)
    crowded, ordinary = portions_of(number_of, rows * top, bound, slope, True), portions_of(number_of, rows * top, bound, slope, False)
    places = jnp.arange(number_of)

    def named(lengths, offset_by):
        used = int((lengths > 0).sum())
        fixed = max(1, used // 4)
        moved = fixed + (places - fixed + offset_by * (used - fixed)) % max(1, number_of - fixed)
        return jnp.zeros((number_of,), jnp.int32).at[ranking[jnp.where(places < fixed, places, moved)]].set(jnp.asarray(lengths, jnp.int32))

    lengths = jnp.where(number % 4 == 0, named(crowded, number // 4), named(ordinary, number - number // 4 - 1))
    mixed = jax.random.permutation(jax.random.fold_in(own, 3), number_of)
    source_of, sink = mixed[0:number_of // 2 * 2:2], mixed[1:number_of // 2 * 2:2]
    room = jnp.minimum(lengths[source_of] - 1, bound - lengths[sink]) // 2
    room = jnp.where((source_of == ranking[0]) | (sink == ranking[0]) | (lengths[sink] == 0), 0, jnp.maximum(room, 0))
    moved = jax.random.randint(jax.random.fold_in(own, 4), (number_of // 2,), 0, 1 << 20) % (room + 1)
    lengths = lengths.at[source_of].add(-moved).at[sink].add(moved)
    labels = jnp.searchsorted(jnp.cumsum(lengths), jnp.arange(rows * top), side="right").astype(jnp.int32)
    listing = labels.reshape(top, rows).T
    listing = listing[jax.random.permutation(jax.random.fold_in(own, 1), rows)]
    offset_by = jax.random.randint(jax.random.fold_in(own, 2), (rows, 1), 0, top)
    return jnp.take_along_axis(listing, (jnp.arange(top)[None, :] + offset_by) % top, axis=1)


def portions_of(count, total, bound, lean, full):
    loads = [(1 << 20) // math.isqrt(standing ** lean) + 1 for standing in range(1, count + 1)]
    largest = bound if full else min(bound, max(-(-total // count), total * loads[0] // sum(loads)))
    least = 1 if total - largest >= count - 1 else 0
    counts, rest = [largest] + [least] * (count - 1), total - largest - least * (count - 1)
    while rest > 0:
        free = [i for i in range(1, count) if counts[i] < largest] or [i for i in range(1, count) if counts[i] < bound]
        mass, left = sum([loads[i] for i in free]), rest
        for i in free:
            more = min(bound - counts[i], max(1, left * loads[i] // mass), rest)
            counts[i] = counts[i] + more
            rest = rest - more
    return np.array(counts)


def gaussian(stream_key, shape, width, reach, split=(), kind=jnp.bfloat16):
    values = width * jax.random.normal(stream_key, shape, jnp.float32)
    if split:
        values = values * level_of(stream_key, shape, split, -0.22, 0.18)
    return jnp.clip(values, -reach, reach).astype(kind)


def setup_inputs(seed: int = 0) -> dict:
    key_of = jax.random.split(jax.random.key(seed), 8)
    tokens = gaussian(key_of[0], (TOKENS, D), 1.0, 6.0, ((0, 256),))
    d_out = gaussian(key_of[1], (TOKENS, D), 1.0, 6.0, ((0, 256),))
    route_probs = jnp.clip(jnp.exp(math.log(0.3984375) - 2.9969585 * jax.random.uniform(key_of[2], (TOKENS, TOP), jnp.float32) ** level_of(key_of[2], (TOKENS, TOP), ((0, 256),), -0.2, 0.2)), 0.019897461, 0.3984375).astype(jnp.bfloat16)
    routes_keys = jax.random.split(jax.random.fold_in(key_of[3], 1), TOKENS // TOK_DEV)
    routes_turns = jax.random.permutation(jax.random.fold_in(key_of[3], 3), TOKENS // TOK_DEV)
    routes = jax.vmap(lambda own, number: deal_out(jax.random.fold_in(key_of[3], 2), own, number, TOK_DEV, EXPERTS, TOP, CAP, 1))(routes_keys, routes_turns).reshape((TOKENS, TOP))
    w_gate = gaussian(key_of[4], (EXPERTS, D, FFW), D ** -0.5, 0.125, ((0, 64),))
    w_up = gaussian(key_of[5], (EXPERTS, D, FFW), D ** -0.5, 0.125, ((0, 64),))
    w_down = gaussian(key_of[6], (EXPERTS, FFW, D), FFW ** -0.5, 0.25, ((0, 64),))
    return dict(tokens=tokens, d_out=d_out, route_probs=route_probs, routes=routes, w_gate=w_gate, w_up=w_up, w_down=w_down)


def expert_rows(x_rows, dy_rows, prob_rows, gate_w, up_w, down_w):
    gate_val = jnp.dot(x_rows, gate_w, preferred_element_type=jnp.float32)
    up_val = jnp.dot(x_rows, up_w, preferred_element_type=jnp.float32)
    sigmoid_g = jax.nn.sigmoid(gate_val)
    silu_g = gate_val * sigmoid_g
    hidden = (silu_g * up_val).astype(jnp.bfloat16)
    back_hidden = jnp.dot(dy_rows, down_w.T, preferred_element_type=jnp.float32)
    prob_rows_grad = jnp.sum(hidden.astype(jnp.float32) * back_hidden, axis=1).astype(jnp.bfloat16)
    prob_col = prob_rows.astype(jnp.float32)[:, None]
    scaled_dy = (prob_col * dy_rows.astype(jnp.float32)).astype(jnp.bfloat16)
    d_hidden = prob_col * back_hidden
    d_gate = (d_hidden * up_val * sigmoid_g * (1.0 + gate_val * (1.0 - sigmoid_g))).astype(jnp.bfloat16)
    d_up = (d_hidden * silu_g).astype(jnp.bfloat16)
    d_rows = (jnp.dot(d_gate, gate_w.T, preferred_element_type=jnp.float32)
              + jnp.dot(d_up, up_w.T, preferred_element_type=jnp.float32)).astype(jnp.bfloat16)
    grad_gate_part = jnp.dot(x_rows.T, d_gate, preferred_element_type=jnp.float32)
    grad_up_part = jnp.dot(x_rows.T, d_up, preferred_element_type=jnp.float32)
    grad_down_part = jnp.dot(hidden.T, scaled_dy, preferred_element_type=jnp.float32)
    return d_rows, prob_rows_grad, (grad_gate_part, grad_up_part, grad_down_part)


def reference(tokens, d_out, route_probs, routes, w_gate, w_up, w_down):
    devices_all = N_DP * N_EXPERT
    pairs = TOK_DEV * TOP
    sentinel = TOKENS * TOP
    flat_routes = routes.reshape(devices_all, pairs).astype(jnp.int32)
    onehot = (flat_routes[:, :, None] == jnp.arange(EXPERTS, dtype=jnp.int32)[None, None, :]).astype(jnp.int32)
    before = jnp.cumsum(onehot, axis=1) - onehot
    slot_index = jnp.sum(before * onehot, axis=2).astype(jnp.int32)
    device_ids = jnp.broadcast_to(jnp.arange(devices_all, dtype=jnp.int32)[:, None], (devices_all, pairs))
    group_ids = device_ids // N_EXPERT
    source_ids = device_ids % N_EXPERT
    pair_ids = device_ids * pairs + jnp.arange(pairs, dtype=jnp.int32)[None, :]
    table = jnp.full((N_DP, EXPERTS, N_EXPERT * CAP), sentinel, jnp.int32)
    table = table.at[group_ids, flat_routes, source_ids * CAP + slot_index].set(pair_ids)
    blank_row = jnp.zeros((1, D), jnp.bfloat16)
    tok_pad = jnp.concatenate([tokens, blank_row], axis=0)
    dout_pad = jnp.concatenate([d_out, blank_row], axis=0)
    prob_pad = jnp.concatenate([route_probs.reshape(sentinel), jnp.zeros((1,), jnp.bfloat16)])

    def one_expert(carry, inputs):
        tok_acc, prob_acc = carry
        expert_id, gate_w, up_w, down_w = inputs
        expert_table = lax.dynamic_index_in_dim(table, expert_id, 1, keepdims=False)
        grad_sums = [jnp.zeros((D, FFW), jnp.float32), jnp.zeros((D, FFW), jnp.float32), jnp.zeros((FFW, D), jnp.float32)]
        for group_index in range(N_DP):
            slot_rows = expert_table[group_index]
            owner = slot_rows // TOP
            d_rows, prob_rows_grad, parts = expert_rows(tok_pad[owner], dout_pad[owner], prob_pad[slot_rows], gate_w, up_w, down_w)
            tok_acc = tok_acc.at[owner].add(d_rows.astype(jnp.float32))
            prob_acc = prob_acc.at[slot_rows].add(prob_rows_grad.astype(jnp.float32))
            grad_sums = [total + lax.optimization_barrier(part.astype(jnp.bfloat16)).astype(jnp.float32)
                         for total, part in zip(grad_sums, parts)]
        return (tok_acc, prob_acc), tuple(total.astype(jnp.bfloat16) for total in grad_sums)

    start = (jnp.zeros((TOKENS + 1, D), jnp.float32), jnp.zeros((sentinel + 1,), jnp.float32))
    (tok_acc, prob_acc), grads = lax.scan(one_expert, start, (jnp.arange(EXPERTS, dtype=jnp.int32), w_gate, w_up, w_down))
    d_tokens = tok_acc[:TOKENS].astype(jnp.bfloat16)
    d_probs = prob_acc[:sentinel].reshape(TOKENS, TOP).astype(jnp.bfloat16)
    return d_tokens, d_probs, grads[0], grads[1], grads[2]
```

```python
import jax
import jax.numpy as jnp
from jax import lax
from jax.experimental import pallas as pl
from jax.experimental.pallas import tpu as pltpu
from jax.sharding import PartitionSpec as P

MESH = pl.DeviceIdType.MESH
BF, F32 = jnp.bfloat16, jnp.float32

D = 2048
F = 512
T = 128
TOP = 8
NP = 16
NZ = 8
SLOTS = 16
MAIN = NP * SLOTS
ROWS = MAIN + NP
LANE = 128
WIDE = D + LANE
BACK = WIDE + LANE
NCH = 4
OTHERS = MAIN - SLOTS
QD = D // 4


def dot(left, right, left_dim=1, right_dim=0):
    return lax.dot_general(
        left, right, (((left_dim,), (right_dim,)), ((), ())), preferred_element_type=F32
    )


def iota(shape, dim):
    return lax.broadcasted_iota(jnp.int32, shape, dim)


def kernel(
    tok_hbm, dout_hbm, prob_ref, routes_ref, wg_hbm, wu_hbm, wd_hbm,
    dtok_ref, dprob_ref, gout_ref,
    zl_ref, meta_all, meta, onehot, perm, expand, snd, rxz, wts, rows_x, rows_z, extra,
    dall, rrcv, zsnd, zrcv, acc, core_rcv, low_rcv,
    load_sem, zs_sem, zr_sem, ms_sem, mr_sem, as_sem, ar_sem, bs_sem, br_sem,
    ts_sem, tr_sem, cs_sem, cr_sem, ls_sem, lr_sem,
):
    dp, ex = lax.axis_index("dp"), lax.axis_index("expert")
    core, low = lax.rem(dp, 2), lax.div(dp, 2)
    high, me = lax.rem(ex, 4), lax.div(ex, 4)
    z = high * 2 + low
    sign = 1 - 2 * low

    def column(offset):
        there = lax.rem(z + offset + 2 * NZ, NZ)
        return (lax.rem(there, 2) * 2 + core, me * 4 + lax.div(there, 2))

    def plane(number):
        return (dp, number * 4 + high)

    other_core = (low * 2 + 1 - core, ex)
    other_low = ((1 - low) * 2 + core, ex)

    def remote(src, dst, send, recv, device):
        return pltpu.make_async_remote_copy(
            src_ref=src, dst_ref=dst, send_sem=send, recv_sem=recv,
            device_id=device, device_id_type=MESH,
        )

    def wait_for(ref, sem):
        pltpu.make_async_copy(ref, ref, sem).wait()

    loads = [
        pltpu.make_async_copy(tok_hbm, zl_ref.at[0, 0], load_sem.at[0]),
        pltpu.make_async_copy(dout_hbm, zl_ref.at[1, 0], load_sem.at[1]),
        pltpu.make_async_copy(wg_hbm, wts.at[0], load_sem.at[2]),
        pltpu.make_async_copy(wu_hbm, wts.at[1], load_sem.at[3]),
    ] + [
        pltpu.make_async_copy(wd_hbm.at[:, QD * r : QD * (r + 1)], wts.at[2, r], load_sem.at[4 + r])
        for r in range(4)
    ]
    for load in loads:
        load.start()

    barrier = pltpu.get_barrier_semaphore()

    def greet(device):
        pl.semaphore_signal(barrier, inc=1, device_id=device, device_id_type=MESH)

    def greet_plane(step, carry):
        greet(plane(lax.rem(me + step, NP)))
        return carry

    lax.fori_loop(1, NP, greet_plane, 0)
    for offset in (-sign, -3 * sign, 2 * sign, -2 * sign):
        greet(column(offset))
    greet(other_core)
    greet(other_low)
    pl.semaphore_wait(barrier, NP - 1 + 6)

    for a in range(2):
        loads[a].wait()
        remote(
            zl_ref.at[a, 0], zl_ref.at[a, 1], zs_sem.at[a, 0], zr_sem.at[a, 0], column(-sign)
        ).start()

    routes = routes_ref[...]
    rank = (routes & 3) * NP + (routes >> 2)
    probs = prob_ref[...].astype(F32)
    lane = iota((T, LANE), 1)
    named = jnp.zeros((T, LANE), F32)
    weight = jnp.zeros((T, LANE), F32)
    for k in range(TOP):
        hit = rank[:, k : k + 1] == lane
        named = named + jnp.where(hit, 1.0, 0.0)
        weight = weight + jnp.where(hit, probs[:, k : k + 1], 0.0)
    earlier = jnp.where(iota((T, T), 1) < iota((T, T), 0), 1.0, 0.0).astype(BF)
    slot = dot(earlier, named.astype(BF))
    slot = jnp.where(named > 0.5, slot, -1.0).T
    weight = weight.T
    for h in range(4):
        meta_all[32 * h : 32 * h + 16, :] = slot[16 * h : 16 * h + 16].astype(BF)
        meta_all[32 * h + 16 : 32 * h + 32, :] = weight[16 * h : 16 * h + 16].astype(BF)
    for j, offset in enumerate((-sign, 2 * sign, -3 * sign)):
        there = lax.div(lax.rem(z + offset + 2 * NZ, NZ), 2)
        remote(
            meta_all.at[pl.ds(pl.multiple_of(there * 32, 32), 32), :],
            meta.at[j + 1], ms_sem.at[j], mr_sem.at[j], column(offset),
        ).start()
    meta[0] = meta_all[pl.ds(pl.multiple_of(high * 32, 32), 32), :]

    row, col = iota((MAIN, MAIN), 0), iota((MAIN, MAIN), 1)
    perm[...] = jnp.where(col == (row & 15) * 16 + (row >> 4), 1.0, 0.0).astype(BF)
    expand[...] = jnp.where(iota((MAIN, NP), 0) >> 4 == iota((MAIN, NP), 1), 1.0, 0.0).astype(BF)

    def to_tiles(value):
        stacked = jnp.concatenate([value[:, LANE * j : LANE * (j + 1)] for j in range(16)], axis=0)
        return dot(perm[...], stacked).astype(BF)

    def from_tiles(tiles):
        stacked = dot(perm[...], tiles).astype(BF)
        return [stacked[16 * j : 16 * j + 16] for j in range(16)]

    def dispatch(c):
        @pl.when(c >= 1)
        def _():
            wait_for(meta.at[c], mr_sem.at[c - 1])

        slots, weights = meta[c, 0:16, :], meta[c, 16:32, :]
        at_slot = dot(expand[...], slots) == (iota((MAIN, T), 0) & 15).astype(F32)
        last = slots.astype(F32) == float(SLOTS)
        onehot[c, 0, 0:MAIN, :] = jnp.where(at_slot, 1.0, 0.0).astype(BF)
        onehot[c, 0, MAIN:ROWS, :] = jnp.where(last, 1.0, 0.0).astype(BF)
        onehot[c, 1, 0:MAIN, :] = jnp.where(at_slot, dot(expand[...], weights), 0.0).astype(BF)
        onehot[c, 1, MAIN:ROWS, :] = jnp.where(last, weights.astype(F32), 0.0).astype(BF)

        for a in range(2):
            @pl.when(c >= 1)
            def _():
                wait_for(zl_ref.at[a, c], zr_sem.at[a, c - 1])

            @pl.when(c == 1)
            def _():
                remote(
                    zl_ref.at[a, 0], zl_ref.at[a, 2], zs_sem.at[a, 1], zr_sem.at[a, 1],
                    column(2 * sign),
                ).start()

            @pl.when(c == 2)
            def _():
                remote(
                    zl_ref.at[a, 1], zl_ref.at[a, 3], zs_sem.at[a, 2], zr_sem.at[a, 2],
                    column(2 * sign),
                ).start()

            tail = []
            for r in range(4):
                packed = dot(onehot[c, a], zl_ref[a, c, :, QD * r : QD * (r + 1)]).astype(BF)
                snd[a, c, :, QD * r : QD * (r + 1)] = packed[0:MAIN]
                tail.append(packed[MAIN:ROWS])
            snd[a, c, :, D:WIDE] = to_tiles(jnp.concatenate(tail, axis=1))

            mine = pl.ds(pl.multiple_of(me * SLOTS, SLOTS), SLOTS)

            def send(step, carry):
                to = lax.rem(me + step, NP)
                remote(
                    snd.at[a, c, pl.ds(pl.multiple_of(to * SLOTS, SLOTS), SLOTS), 0:WIDE],
                    rxz.at[a, c, mine, :], as_sem.at[a, c], ar_sem.at[a, c], plane(to),
                ).start()
                return carry

            lax.fori_loop(1, NP, send, 0)
            rxz[a, c, mine, :] = snd[a, c, mine, 0:WIDE]

    def expert(c):
        here = pl.ds(pl.multiple_of(c * MAIN, MAIN), MAIN)
        spare = pl.ds(pl.multiple_of(NCH * MAIN + c * NP, NP), NP)
        side = pl.ds(pl.multiple_of(c * NP, NP), NP)
        for a, rows in ((0, rows_x), (1, rows_z)):
            wait_for(rxz.at[a, c, 0:OTHERS, :], ar_sem.at[a, c])
            rows[0:MAIN, 0:D] = rxz[a, c, :, 0:D]
            for j, block in enumerate(from_tiles(rxz[a, c, :, D:WIDE])):
                rows[MAIN:ROWS, LANE * j : LANE * (j + 1)] = block
                extra[a, side, LANE * j : LANE * (j + 1)] = block
        gate = dot(rows_x[:, 0:QD], wts[0, 0])
        up = dot(rows_x[:, 0:QD], wts[1, 0])
        back = dot(rows_z[:, 0:QD], wts[2, 0], 1, 1)
        for r in range(1, 4):
            part = slice(QD * r, QD * (r + 1))
            gate = gate + dot(rows_x[:, part], wts[0, r])
            up = up + dot(rows_x[:, part], wts[1, r])
            back = back + dot(rows_z[:, part], wts[2, r], 1, 1)
        sig = jax.nn.sigmoid(gate)
        silu = gate * sig
        hidden = (silu * up).astype(BF)
        prob = jnp.sum(hidden.astype(F32) * back, axis=1, keepdims=True)
        d_gate = (back * up * sig * (1.0 + gate * (1.0 - sig))).astype(BF)
        d_up = (back * silu).astype(BF)
        for g, value in ((0, d_gate), (1, d_up), (2, hidden)):
            dall[g, here, :] = value[0:MAIN]
            dall[g, spare, :] = value[MAIN:ROWS]
        wait_for(snd.at[0, c, 0:OTHERS, 0:WIDE], as_sem.at[0, c])
        tail = []
        for r in range(4):
            d_rows = (dot(d_gate, wts[0, r], 1, 1) + dot(d_up, wts[1, r], 1, 1)).astype(BF)
            snd[0, c, :, QD * r : QD * (r + 1)] = d_rows[0:MAIN]
            tail.append(d_rows[MAIN:ROWS])
        snd[0, c, :, D:WIDE] = to_tiles(jnp.concatenate(tail, axis=1))
        prob_main = jnp.broadcast_to(prob[0:MAIN], (MAIN, LANE))
        prob_last = dot(expand[...], jnp.broadcast_to(prob[MAIN:ROWS], (NP, LANE)).astype(BF))
        snd[0, c, :, WIDE:BACK] = jnp.where(
            iota((MAIN, LANE), 1) < 64, prob_main, prob_last
        ).astype(BF)

        mine = pl.ds(pl.multiple_of(me * SLOTS, SLOTS), SLOTS)

        def send(step, carry):
            to = lax.rem(me + step, NP)
            remote(
                snd.at[0, c, pl.ds(pl.multiple_of(to * SLOTS, SLOTS), SLOTS), :],
                rrcv.at[c, mine, :], bs_sem.at[c], br_sem.at[c], plane(to),
            ).start()
            return carry

        lax.fori_loop(1, NP, send, 0)
        rrcv[c, mine, :] = snd[0, c, mine, :]

    def combine(c):
        wait_for(rrcv.at[c, 0:OTHERS, :], br_sem.at[c])
        rows_x[0:MAIN, 0:D] = rrcv[c, :, 0:D]
        for j, block in enumerate(from_tiles(rrcv[c, :, D:WIDE])):
            rows_x[MAIN:ROWS, LANE * j : LANE * (j + 1)] = block
        tile = rrcv[c, :, WIDE:BACK]
        owner = iota((MAIN, LANE), 0) >> 4
        rows_x[0:MAIN, D:WIDE] = jnp.where(
            iota((MAIN, LANE), 1) == owner + high * NP, tile.astype(F32), 0.0
        ).astype(BF)
        first = jnp.where(iota((NP, MAIN), 1) == iota((NP, MAIN), 0) * SLOTS, 1.0, 0.0).astype(BF)
        rows_x[MAIN:ROWS, D:WIDE] = jnp.where(
            iota((NP, LANE), 1) == iota((NP, LANE), 0) + high * NP + 64, dot(first, tile), 0.0
        ).astype(BF)
        return dot(onehot[c, 0], rows_x[...], 0, 0)

    def combine_far(c):
        zsnd[c - 1] = combine(c).astype(BF)
        remote(
            zsnd.at[c - 1], zrcv.at[c - 1], ts_sem.at[c - 1], tr_sem.at[c - 1], column(-c * sign)
        ).start()

    dispatch(0)
    for load in loads[2:]:
        load.wait()

    def step(c, carry):
        @pl.when(c < NCH - 1)
        def _():
            dispatch(c + 1)

        expert(c)

        @pl.when(c >= 2)
        def _():
            combine_far(c - 1)

        return carry

    lax.fori_loop(0, NCH, step, 0)

    def weight_gradient(g, r):
        a = lax.div(g, 2)
        part = pl.ds(pl.multiple_of(r * QD, QD), QD)
        main = dall[g, 0 : NCH * MAIN, :]
        total = dot(main, rxz[a, :, :, part].reshape(NCH * MAIN, QD), 0, 0)
        total = total + dot(dall[g, NCH * MAIN : NCH * ROWS, :], extra[a, :, part], 0, 0)
        wts[g, r] = total.astype(BF)

    def to_core(i, carry):
        g, half = lax.div(i, 2), lax.rem(i, 2)
        r = half * 2 + 1 - core
        weight_gradient(g, r)
        remote(
            wts.at[g, r], core_rcv.at[g, half], cs_sem.at[g, half], cr_sem.at[g, half], other_core
        ).start()
        return carry

    lax.fori_loop(0, 6, to_core, 0)

    def to_low(g, carry):
        r = (1 - low) * 2 + core
        weight_gradient(g, r)
        wait_for(core_rcv.at[g, 1 - low], cr_sem.at[g, 1 - low])
        wts[g, r] = (wts[g, r].astype(F32) + core_rcv[g, 1 - low].astype(F32)).astype(BF)
        remote(wts.at[g, r], low_rcv.at[g], ls_sem.at[g], lr_sem.at[g], other_low).start()
        return carry

    lax.fori_loop(0, 3, to_low, 0)
    combine_far(NCH - 1)

    def to_own(g, carry):
        weight_gradient(g, low * 2 + core)
        return carry

    lax.fori_loop(0, 3, to_own, 0)
    acc[...] = combine(0)

    def finish(g, carry):
        r = low * 2 + core
        wait_for(core_rcv.at[g, low], cr_sem.at[g, low])
        wait_for(low_rcv.at[g], lr_sem.at[g])
        gout_ref[g] = (
            wts[g, r].astype(F32) + core_rcv[g, low].astype(F32) + low_rcv[g].astype(F32)
        ).astype(BF)
        return carry

    lax.fori_loop(0, 3, finish, 0)
    for j in range(NCH - 1):
        wait_for(zrcv.at[j], tr_sem.at[j])
    total = acc[...]
    for j in range(NCH - 1):
        total = total + zrcv[j].astype(F32)
    dtok_ref[...] = total[:, 0:D].astype(BF)
    entries = total[:, D:WIDE]
    d_probs = jnp.zeros((T, TOP), F32)
    for k in range(TOP):
        entry = jnp.sum(
            jnp.where((lane & 63) == rank[:, k : k + 1], entries, 0.0), axis=1, keepdims=True
        )
        d_probs = d_probs + jnp.where(iota((T, TOP), 1) == k, entry, 0.0)
    dprob_ref[...] = (d_probs / probs).astype(BF)

    for j in range(NCH - 1):
        for a in range(2):
            wait_for(zl_ref.at[a, 0], zs_sem.at[a, j])
        wait_for(meta.at[0], ms_sem.at[j])
        wait_for(zsnd.at[j], ts_sem.at[j])
    for c in range(NCH):
        wait_for(snd.at[1, c, 0:OTHERS, 0:WIDE], as_sem.at[1, c])
        wait_for(snd.at[0, c, 0:OTHERS, :], bs_sem.at[c])
    for g in range(3):
        for half in range(2):
            wait_for(core_rcv.at[g, half], cs_sem.at[g, half])
        wait_for(low_rcv.at[g], ls_sem.at[g])


def shards(tokens, d_out, route_probs, routes, w_gate, w_up, w_down):
    dma = pltpu.SemaphoreType.DMA
    anywhere, vmem = pl.BlockSpec(memory_space=pl.ANY), pl.BlockSpec(memory_space=pltpu.VMEM)
    d_tokens, d_probs, grads = pl.pallas_call(
        kernel,
        out_shape=(
            jax.ShapeDtypeStruct((T, D), BF),
            jax.ShapeDtypeStruct((T, TOP), BF),
            jax.ShapeDtypeStruct((3, F, QD), BF),
        ),
        in_specs=[anywhere, anywhere, vmem, vmem, anywhere, anywhere, anywhere],
        out_specs=(vmem, vmem, vmem),
        scratch_shapes=[
            pltpu.VMEM((2, NCH, T, D), BF),
            pltpu.VMEM((T, LANE), BF),
            pltpu.VMEM((NCH, 32, LANE), BF),
            pltpu.VMEM((NCH, 2, ROWS, T), BF),
            pltpu.VMEM((MAIN, MAIN), BF),
            pltpu.VMEM((MAIN, NP), BF),
            pltpu.VMEM((2, NCH, MAIN, BACK), BF),
            pltpu.VMEM((2, NCH, MAIN, WIDE), BF),
            pltpu.VMEM((3, 4, F, QD), BF),
            pltpu.VMEM((ROWS, WIDE), BF),
            pltpu.VMEM((ROWS, D), BF),
            pltpu.VMEM((2, NCH * NP, D), BF),
            pltpu.VMEM((3, NCH * ROWS, F), BF),
            pltpu.VMEM((NCH, MAIN, BACK), BF),
            pltpu.VMEM((NCH - 1, T, WIDE), BF),
            pltpu.VMEM((NCH - 1, T, WIDE), BF),
            pltpu.VMEM((T, WIDE), F32),
            pltpu.VMEM((3, 2, F, QD), BF),
            pltpu.VMEM((3, F, QD), BF),
            dma((8,)),
            dma((2, 3)), dma((2, 3)), dma((3,)), dma((3,)),
            dma((2, NCH)), dma((2, NCH)), dma((NCH,)), dma((NCH,)),
            dma((3,)), dma((3,)), dma((3, 2)), dma((3, 2)), dma((3,)), dma((3,)),
        ],
        compiler_params=pltpu.CompilerParams(
            collective_id=0, has_side_effects=True, vmem_limit_bytes=62 << 20
        ),
    )(
        tokens, d_out, route_probs, routes,
        w_gate.reshape(4, QD, F), w_up.reshape(4, QD, F), w_down.reshape(F, D),
    )
    return (
        d_tokens,
        d_probs,
        grads[0].T[None],
        grads[1].T[None],
        grads[2][None],
    )


def solution(mesh):
    return jax.shard_map(
        shards,
        mesh=mesh,
        in_specs=(
            P(("dp", "expert"), None),
            P(("dp", "expert"), None),
            P(("dp", "expert"), None),
            P(("dp", "expert"), None),
            P("expert", None, None),
            P("expert", None, None),
            P("expert", None, None),
        ),
        out_specs=(
            P(("dp", "expert"), None),
            P(("dp", "expert"), None),
            P("expert", "dp", None),
            P("expert", "dp", None),
            P("expert", None, "dp"),
        ),
        check_vma=False,
    )
```

```python
import jax
import jax.numpy as jnp
from jax import lax
from jax.experimental import pallas as pl
from jax.experimental.pallas import tpu as pltpu
from jax.sharding import PartitionSpec as P

MESH = pl.DeviceIdType.MESH
BF, F32 = jnp.bfloat16, jnp.float32

D = 2048
F = 512
T = 128
TOP = 8
NP = 16
NZ = 8
SLOTS = 16
MAIN = NP * SLOTS
ROWS = MAIN + NP
LANE = 128
WIDE = D + LANE
BACK = WIDE + LANE
NCH = 4
OTHERS = MAIN - SLOTS
QD = D // 4


def dot(left, right, left_dim=1, right_dim=0):
    return lax.dot_general(
        left, right, (((left_dim,), (right_dim,)), ((), ())), preferred_element_type=F32
    )


def iota(shape, dim):
    return lax.broadcasted_iota(jnp.int32, shape, dim)


def kernel(
    tok_hbm, dout_hbm, prob_ref, routes_ref, wg_hbm, wu_hbm, wd_hbm,
    dtok_ref, dprob_ref, ggate_ref, gup_ref, gdown_ref,
    zl_ref, meta_all, meta, onehot, perm, expand, snd, rxz, wts, rows_x, rows_z, extra,
    dall, rrcv, zsnd, zrcv, acc, core_rcv, low_rcv,
    load_sem, zs_sem, zr_sem, ms_sem, mr_sem, as_sem, ar_sem, bs_sem, br_sem,
    ts_sem, tr_sem, cs_sem, cr_sem, ls_sem, lr_sem,
):
    dp, ex = lax.axis_index("dp"), lax.axis_index("expert")
    core, low = lax.rem(dp, 2), lax.div(dp, 2)
    high, me = lax.rem(ex, 4), lax.div(ex, 4)
    z = high * 2 + low
    sign = 1 - 2 * low

    def column(offset):
        there = lax.rem(z + offset + 2 * NZ, NZ)
        return (lax.rem(there, 2) * 2 + core, me * 4 + lax.div(there, 2))

    def around(step):
        there_x = lax.rem(lax.div(me, 4) + lax.div(step, 4), 4)
        return there_x * 4 + lax.rem(lax.rem(me, 4) + lax.rem(step, 4), 4)

    def plane(number):
        return (dp, number * 4 + high)

    other_core = (low * 2 + 1 - core, ex)
    other_low = ((1 - low) * 2 + core, ex)

    def remote(src, dst, send, recv, device):
        return pltpu.make_async_remote_copy(
            src_ref=src, dst_ref=dst, send_sem=send, recv_sem=recv,
            device_id=device, device_id_type=MESH,
        )

    def wait_for(ref, sem):
        pltpu.make_async_copy(ref, ref, sem).wait()

    loads = [
        pltpu.make_async_copy(tok_hbm, zl_ref.at[0, 0], load_sem.at[0]),
        pltpu.make_async_copy(dout_hbm, zl_ref.at[1, 0], load_sem.at[1]),
        pltpu.make_async_copy(wg_hbm, wts.at[0], load_sem.at[2]),
        pltpu.make_async_copy(wu_hbm, wts.at[1], load_sem.at[3]),
    ] + [
        pltpu.make_async_copy(wd_hbm.at[:, QD * r : QD * (r + 1)], wts.at[2, r], load_sem.at[4 + r])
        for r in range(4)
    ]
    for load in loads:
        load.start()

    barrier = pltpu.get_barrier_semaphore()

    def greet(device):
        pl.semaphore_signal(barrier, inc=1, device_id=device, device_id_type=MESH)

    def greet_plane(step, carry):
        greet(plane(lax.rem(me + step, NP)))
        return carry

    lax.fori_loop(1, NP, greet_plane, 0)
    for offset in (-sign, -3 * sign, 2 * sign, -2 * sign):
        greet(column(offset))
    greet(other_core)
    greet(other_low)
    pl.semaphore_wait(barrier, NP - 1 + 6)

    def along_z(c, a):
        remote(
            zl_ref.at[a, jnp.where(c == 3, 1, 0)], zl_ref.at[a, c],
            zs_sem.at[a, c - 1], zr_sem.at[a, c - 1], column(jnp.where(c == 1, -sign, 2 * sign)),
        ).start()

    loads[0].wait()
    along_z(1, 0)
    loads[1].wait()

    routes = routes_ref[...]
    rank = (routes & 3) * NP + (routes >> 2)
    probs = prob_ref[...].astype(F32)
    number = iota((64, T), 0)
    named = jnp.zeros((64, T), F32)
    weight = jnp.zeros((64, T), F32)
    for k in range(TOP):
        hit = rank[k : k + 1, :] == number
        named = named + jnp.where(hit, 1.0, 0.0)
        weight = weight + jnp.where(hit, probs[k : k + 1, :], 0.0)
    earlier = jnp.where(iota((T, T), 0) < iota((T, T), 1), 1.0, 0.0).astype(BF)
    slot = jnp.where(named > 0.5, dot(named.astype(BF), earlier), -1.0)
    for h in range(4):
        meta_all[32 * h : 32 * h + 16, :] = slot[16 * h : 16 * h + 16].astype(BF)
        meta_all[32 * h + 16 : 32 * h + 32, :] = weight[16 * h : 16 * h + 16].astype(BF)
    for j, offset in enumerate((-sign, 2 * sign, -3 * sign)):
        there = lax.div(lax.rem(z + offset + 2 * NZ, NZ), 2)
        remote(
            meta_all.at[pl.ds(pl.multiple_of(there * 32, 32), 32), :],
            meta.at[j + 1], ms_sem.at[j], mr_sem.at[j], column(offset),
        ).start()
    meta[0] = meta_all[pl.ds(pl.multiple_of(high * 32, 32), 32), :]

    row, col = iota((MAIN, MAIN), 0), iota((MAIN, MAIN), 1)
    perm[...] = jnp.where(col == (row & 15) * 16 + (row >> 4), 1.0, 0.0).astype(BF)
    expand[...] = jnp.where(iota((MAIN, NP), 0) >> 4 == iota((MAIN, NP), 1), 1.0, 0.0).astype(BF)

    def to_tiles(value):
        stacked = jnp.concatenate([value[:, LANE * j : LANE * (j + 1)] for j in range(16)], axis=0)
        return dot(perm[...], stacked).astype(BF)

    def from_tiles(tiles):
        stacked = dot(perm[...], tiles).astype(BF)
        return [stacked[16 * j : 16 * j + 16] for j in range(16)]

    def dispatch(c):
        @pl.when(c >= 1)
        def _():
            wait_for(meta.at[c], mr_sem.at[c - 1])

        slots, weights = meta[c, 0:16, :], meta[c, 16:32, :]
        at_slot = dot(expand[...], slots) == (iota((MAIN, T), 0) & 15).astype(F32)
        last = slots.astype(F32) == float(SLOTS)
        onehot[c, 0, 0:MAIN, :] = jnp.where(at_slot, 1.0, 0.0).astype(BF)
        onehot[c, 0, MAIN:ROWS, :] = jnp.where(last, 1.0, 0.0).astype(BF)
        onehot[c, 1, 0:MAIN, :] = jnp.where(at_slot, dot(expand[...], weights), 0.0).astype(BF)
        onehot[c, 1, MAIN:ROWS, :] = jnp.where(last, weights.astype(F32), 0.0).astype(BF)

        def one(a, carry):
            @pl.when(c >= 1)
            def _():
                wait_for(zl_ref.at[a, c], zr_sem.at[a, c - 1])

            @pl.when((c >= 1) & (2 * c + a < 7))
            def _():
                along_z(c + a, 1 - a)

            tail = []
            for r in range(4):
                packed = dot(onehot[c, a], zl_ref[a, c, :, QD * r : QD * (r + 1)]).astype(BF)
                snd[a, c, :, QD * r : QD * (r + 1)] = packed[0:MAIN]
                tail.append(packed[MAIN:ROWS])
            snd[a, c, :, D:WIDE] = to_tiles(jnp.concatenate(tail, axis=1))

            mine = pl.ds(pl.multiple_of(me * SLOTS, SLOTS), SLOTS)

            def send(step, carry):
                to = around(step)
                remote(
                    snd.at[a, c, pl.ds(pl.multiple_of(to * SLOTS, SLOTS), SLOTS), 0:WIDE],
                    rxz.at[a, c, mine, :], as_sem.at[a, c], ar_sem.at[a, c], plane(to),
                ).start()
                return carry

            lax.fori_loop(1, NP, send, 0)
            rxz[a, c, mine, :] = snd[a, c, mine, 0:WIDE]
            return carry

        lax.fori_loop(0, 2, one, 0)

    def expert(c):
        here = pl.ds(pl.multiple_of(c * MAIN, MAIN), MAIN)
        spare = pl.ds(pl.multiple_of(NCH * MAIN + c * NP, NP), NP)
        side = pl.ds(pl.multiple_of(c * NP, NP), NP)
        for a, rows in ((0, rows_x), (1, rows_z)):
            wait_for(rxz.at[a, c, 0:OTHERS, :], ar_sem.at[a, c])
            rows[0:MAIN, 0:D] = rxz[a, c, :, 0:D]
            for j, block in enumerate(from_tiles(rxz[a, c, :, D:WIDE])):
                rows[MAIN:ROWS, LANE * j : LANE * (j + 1)] = block
                extra[a, side, LANE * j : LANE * (j + 1)] = block
        gate = dot(rows_x[:, 0:QD], wts[0, 0])
        up = dot(rows_x[:, 0:QD], wts[1, 0])
        back = dot(rows_z[:, 0:QD], wts[2, 0], 1, 1)
        for r in range(1, 4):
            part = slice(QD * r, QD * (r + 1))
            gate = gate + dot(rows_x[:, part], wts[0, r])
            up = up + dot(rows_x[:, part], wts[1, r])
            back = back + dot(rows_z[:, part], wts[2, r], 1, 1)
        sig = jax.nn.sigmoid(gate)
        silu = gate * sig
        hidden = (silu * up).astype(BF)
        prob = jnp.sum(hidden.astype(F32) * back, axis=1, keepdims=True)
        d_gate = (back * up * sig * (1.0 + gate * (1.0 - sig))).astype(BF)
        d_up = (back * silu).astype(BF)
        for g, value in ((0, d_gate), (1, d_up), (2, hidden)):
            dall[g, here, :] = value[0:MAIN]
            dall[g, spare, :] = value[MAIN:ROWS]
        wait_for(snd.at[0, c, 0:OTHERS, 0:WIDE], as_sem.at[0, c])
        tail = []
        for r in range(4):
            d_rows = (dot(d_gate, wts[0, r], 1, 1) + dot(d_up, wts[1, r], 1, 1)).astype(BF)
            snd[0, c, :, QD * r : QD * (r + 1)] = d_rows[0:MAIN]
            tail.append(d_rows[MAIN:ROWS])
        snd[0, c, :, D:WIDE] = to_tiles(jnp.concatenate(tail, axis=1))
        prob_main = jnp.broadcast_to(prob[0:MAIN], (MAIN, LANE))
        prob_last = dot(expand[...], jnp.broadcast_to(prob[MAIN:ROWS], (NP, LANE)).astype(BF))
        snd[0, c, :, WIDE:BACK] = jnp.where(
            iota((MAIN, LANE), 1) < 64, prob_main, prob_last
        ).astype(BF)

    def give_back(c):
        mine = pl.ds(pl.multiple_of(me * SLOTS, SLOTS), SLOTS)

        def send(step, carry):
            to = around(step)
            remote(
                snd.at[0, c, pl.ds(pl.multiple_of(to * SLOTS, SLOTS), SLOTS), :],
                rrcv.at[c, mine, :], bs_sem.at[c], br_sem.at[c], plane(to),
            ).start()
            return carry

        lax.fori_loop(1, NP, send, 0)
        rrcv[c, mine, :] = snd[0, c, mine, :]

    def combine(c):
        wait_for(rrcv.at[c, 0:OTHERS, :], br_sem.at[c])
        rows_x[0:MAIN, 0:D] = rrcv[c, :, 0:D]
        for j, block in enumerate(from_tiles(rrcv[c, :, D:WIDE])):
            rows_x[MAIN:ROWS, LANE * j : LANE * (j + 1)] = block
        tile = rrcv[c, :, WIDE:BACK]
        owner = iota((MAIN, LANE), 0) >> 4
        rows_x[0:MAIN, D:WIDE] = jnp.where(
            iota((MAIN, LANE), 1) == owner + high * NP, tile.astype(F32), 0.0
        ).astype(BF)
        first = jnp.where(iota((NP, MAIN), 1) == iota((NP, MAIN), 0) * SLOTS, 1.0, 0.0).astype(BF)
        rows_x[MAIN:ROWS, D:WIDE] = jnp.where(
            iota((NP, LANE), 1) == iota((NP, LANE), 0) + high * NP + 64, dot(first, tile), 0.0
        ).astype(BF)
        return dot(onehot[c, 0], rows_x[...], 0, 0)

    def combine_far(c):
        zsnd[c - 1] = combine(c).astype(BF)
        remote(
            zsnd.at[c - 1], zrcv.at[c - 1], ts_sem.at[c - 1], tr_sem.at[c - 1], column(-c * sign)
        ).start()

    dispatch(0)
    for load in loads[2:]:
        load.wait()

    def step(c, carry):
        @pl.when(c < NCH - 1)
        def _():
            dispatch(c + 1)

        @pl.when(c == NCH - 2)
        def _():
            give_back(1)

        expert(c)

        return carry

    lax.fori_loop(0, NCH, step, 0)
    for c in (3, 2, 0):
        give_back(c)

    def weight_gradient(g, r):
        a = lax.div(g, 2)
        part = pl.ds(pl.multiple_of(r * QD, QD), QD)
        main = dall[g, 0 : NCH * MAIN, :]
        total = dot(main, rxz[a, :, :, part].reshape(NCH * MAIN, QD), 0, 0)
        total = total + dot(dall[g, NCH * MAIN : NCH * ROWS, :], extra[a, :, part], 0, 0)
        wts[g, r] = total.astype(BF)

    def to_core(i, carry):
        g, half = lax.div(i, 2), lax.rem(i, 2)
        r = half * 2 + 1 - core
        weight_gradient(g, r)
        remote(
            wts.at[g, r], core_rcv.at[g, half], cs_sem.at[g, half], cr_sem.at[g, half], other_core
        ).start()
        return carry

    lax.fori_loop(0, 6, to_core, 0)

    def to_low(g, carry):
        r = (1 - low) * 2 + core
        weight_gradient(g, r)
        wait_for(core_rcv.at[g, 1 - low], cr_sem.at[g, 1 - low])
        wts[g, r] = (wts[g, r].astype(F32) + core_rcv[g, 1 - low].astype(F32)).astype(BF)
        remote(wts.at[g, r], low_rcv.at[g], ls_sem.at[g], lr_sem.at[g], other_low).start()
        return carry

    lax.fori_loop(0, 3, to_low, 0)
    combine_far(1)

    def to_own(g, carry):
        weight_gradient(g, low * 2 + core)
        return carry

    lax.fori_loop(0, 3, to_own, 0)
    combine_far(3)
    combine_far(2)
    acc[...] = combine(0)

    def finish(g):
        wait_for(core_rcv.at[g, low], cr_sem.at[g, low])
        wait_for(low_rcv.at[g], lr_sem.at[g])
        own = wts[g, low * 2 + core].astype(F32)
        return own + core_rcv[g, low].astype(F32) + low_rcv[g].astype(F32)

    ggate_ref[...] = finish(0).T.astype(BF)
    gup_ref[...] = finish(1).T.astype(BF)
    gdown_ref[...] = finish(2).astype(BF)
    for j in range(NCH - 1):
        wait_for(zrcv.at[j], tr_sem.at[j])
    total = acc[...]
    for j in range(NCH - 1):
        total = total + zrcv[j].astype(F32)
    dtok_ref[...] = total[:, 0:D].astype(BF)
    entries = total[:, D:WIDE].T
    entries = entries[0:64] + entries[64:LANE]
    d_probs = jnp.zeros((TOP, T), F32)
    for k in range(TOP):
        entry = jnp.sum(
            jnp.where(number == rank[k : k + 1, :], entries, 0.0), axis=0, keepdims=True
        )
        d_probs = d_probs + jnp.where(iota((TOP, T), 0) == k, entry, 0.0)
    dprob_ref[...] = (d_probs / probs).astype(BF)

    for j in range(NCH - 1):
        for a in range(2):
            wait_for(zl_ref.at[a, 0], zs_sem.at[a, j])
        wait_for(meta.at[0], ms_sem.at[j])
        wait_for(zsnd.at[j], ts_sem.at[j])
    for c in range(NCH):
        wait_for(snd.at[1, c, 0:OTHERS, 0:WIDE], as_sem.at[1, c])
        wait_for(snd.at[0, c, 0:OTHERS, :], bs_sem.at[c])
    for g in range(3):
        for half in range(2):
            wait_for(core_rcv.at[g, half], cs_sem.at[g, half])
        wait_for(low_rcv.at[g], ls_sem.at[g])


def shards(tokens, d_out, route_probs, routes, w_gate, w_up, w_down):
    dma = pltpu.SemaphoreType.DMA
    anywhere, vmem = pl.BlockSpec(memory_space=pl.ANY), pl.BlockSpec(memory_space=pltpu.VMEM)
    d_tokens, d_probs, g_gate, g_up, g_down = pl.pallas_call(
        kernel,
        out_shape=(
            jax.ShapeDtypeStruct((T, D), BF),
            jax.ShapeDtypeStruct((TOP, T), BF),
            jax.ShapeDtypeStruct((QD, F), BF),
            jax.ShapeDtypeStruct((QD, F), BF),
            jax.ShapeDtypeStruct((F, QD), BF),
        ),
        in_specs=[anywhere, anywhere, vmem, vmem, anywhere, anywhere, anywhere],
        out_specs=(vmem, vmem, vmem, vmem, vmem),
        scratch_shapes=[
            pltpu.VMEM((2, NCH, T, D), BF),
            pltpu.VMEM((T, LANE), BF),
            pltpu.VMEM((NCH, 32, LANE), BF),
            pltpu.VMEM((NCH, 2, ROWS, T), BF),
            pltpu.VMEM((MAIN, MAIN), BF),
            pltpu.VMEM((MAIN, NP), BF),
            pltpu.VMEM((2, NCH, MAIN, BACK), BF),
            pltpu.VMEM((2, NCH, MAIN, WIDE), BF),
            pltpu.VMEM((3, 4, F, QD), BF),
            pltpu.VMEM((ROWS, WIDE), BF),
            pltpu.VMEM((ROWS, D), BF),
            pltpu.VMEM((2, NCH * NP, D), BF),
            pltpu.VMEM((3, NCH * ROWS, F), BF),
            pltpu.VMEM((NCH, MAIN, BACK), BF),
            pltpu.VMEM((NCH - 1, T, WIDE), BF),
            pltpu.VMEM((NCH - 1, T, WIDE), BF),
            pltpu.VMEM((T, WIDE), F32),
            pltpu.VMEM((3, 2, F, QD), BF),
            pltpu.VMEM((3, F, QD), BF),
            dma((8,)),
            dma((2, 3)), dma((2, 3)), dma((3,)), dma((3,)),
            dma((2, NCH)), dma((2, NCH)), dma((NCH,)), dma((NCH,)),
            dma((3,)), dma((3,)), dma((3, 2)), dma((3, 2)), dma((3,)), dma((3,)),
        ],
        compiler_params=pltpu.CompilerParams(
            collective_id=0, has_side_effects=True, vmem_limit_bytes=62 << 20
        ),
    )(
        tokens, d_out, route_probs.T, routes.T,
        w_gate.reshape(4, QD, F), w_up.reshape(4, QD, F), w_down.reshape(F, D),
    )
    return (
        d_tokens,
        d_probs.T,
        g_gate[None],
        g_up[None],
        g_down[None],
    )


def solution(mesh):
    return jax.shard_map(
        shards,
        mesh=mesh,
        in_specs=(
            P(("dp", "expert"), None),
            P(("dp", "expert"), None),
            P(("dp", "expert"), None),
            P(("dp", "expert"), None),
            P("expert", None, None),
            P("expert", None, None),
            P("expert", None, None),
        ),
        out_specs=(
            P(("dp", "expert"), None),
            P(("dp", "expert"), None),
            P("expert", "dp", None),
            P("expert", "dp", None),
            P("expert", None, "dp"),
        ),
        check_vma=False,
    )
```

```python
import jax
import jax.numpy as jnp
from jax import lax
from jax.experimental import pallas as pl
from jax.experimental.pallas import tpu as pltpu
from jax.sharding import PartitionSpec as P

MESH = pl.DeviceIdType.MESH
BF, F32 = jnp.bfloat16, jnp.float32

D = 2048
F = 512
T = 128
TOP = 8
NP = 16
NZ = 8
SLOTS = 16
MAIN = NP * SLOTS
ROWS = MAIN + NP
LANE = 128
WIDE = D + LANE
BACK = WIDE + LANE
NCH = 4
OTHERS = MAIN - SLOTS
QD = D // 4


def dot(left, right, left_dim=1, right_dim=0):
    return lax.dot_general(
        left, right, (((left_dim,), (right_dim,)), ((), ())), preferred_element_type=F32
    )


def iota(shape, dim):
    return lax.broadcasted_iota(jnp.int32, shape, dim)


def kernel(
    tok_hbm, dout_hbm, prob_ref, routes_ref, wg_hbm, wu_hbm, wd_hbm,
    dtok_ref, dprob_ref, ggate_ref, gup_ref, gdown_ref,
    zl_ref, meta_all, meta, onehot, perm, expand, snd, rxz, wts, rows_x, rows_z, extra,
    dall, rrcv, zsnd, zrcv, esnd, ercv, ent, acc, early, gsum, lsnd, core_rcv, low_rcv,
    load_sem, zs_sem, zr_sem, ms_sem, mr_sem, as_sem, ar_sem, bs_sem, br_sem,
    ts_sem, tr_sem, es_sem, er_sem, cs_sem, cr_sem, ls_sem, lr_sem,
):
    dp, ex = lax.axis_index("dp"), lax.axis_index("expert")
    core, low = lax.rem(dp, 2), lax.div(dp, 2)
    high, me = lax.rem(ex, 4), lax.div(ex, 4)
    z = high * 2 + low
    sign = 1 - 2 * low

    def column(offset):
        there = lax.rem(z + offset + 2 * NZ, NZ)
        return (lax.rem(there, 2) * 2 + core, me * 4 + lax.div(there, 2))

    def around(step):
        there_x = lax.rem(lax.div(me, 4) + lax.div(step, 4), 4)
        return there_x * 4 + lax.rem(lax.rem(me, 4) + lax.rem(step, 4), 4)

    def plane(number):
        return (dp, number * 4 + high)

    other_core = (low * 2 + 1 - core, ex)
    other_low = ((1 - low) * 2 + core, ex)

    def remote(src, dst, send, recv, device):
        return pltpu.make_async_remote_copy(
            src_ref=src, dst_ref=dst, send_sem=send, recv_sem=recv,
            device_id=device, device_id_type=MESH,
        )

    def wait_for(ref, sem):
        pltpu.make_async_copy(ref, ref, sem).wait()

    loads = [
        pltpu.make_async_copy(tok_hbm, zl_ref.at[0, 0], load_sem.at[0]),
        pltpu.make_async_copy(dout_hbm, zl_ref.at[1, 0], load_sem.at[1]),
        pltpu.make_async_copy(wg_hbm, wts.at[0], load_sem.at[2]),
        pltpu.make_async_copy(wu_hbm, wts.at[1], load_sem.at[3]),
    ] + [
        pltpu.make_async_copy(wd_hbm.at[:, QD * r : QD * (r + 1)], wts.at[2, r], load_sem.at[4 + r])
        for r in range(4)
    ]
    for load in loads:
        load.start()

    barrier = pltpu.get_barrier_semaphore()

    def greet(device):
        pl.semaphore_signal(barrier, inc=1, device_id=device, device_id_type=MESH)

    def greet_plane(step, carry):
        greet(plane(lax.rem(me + step, NP)))
        return carry

    lax.fori_loop(1, NP, greet_plane, 0)
    for offset in (-sign, -3 * sign, 2 * sign, -2 * sign):
        greet(column(offset))
    greet(other_core)
    greet(other_low)

    routes = routes_ref[...]
    rank = (routes & 3) * NP + (routes >> 2)
    probs = prob_ref[...].astype(F32)
    number = iota((64, T), 0)
    named = jnp.zeros((64, T), F32)
    weight = jnp.zeros((64, T), F32)
    for k in range(TOP):
        hit = rank[k : k + 1, :] == number
        named = named + jnp.where(hit, 1.0, 0.0)
        weight = weight + jnp.where(hit, probs[k : k + 1, :], 0.0)
    earlier = jnp.where(iota((T, T), 0) < iota((T, T), 1), 1.0, 0.0).astype(BF)
    slot = jnp.where(named > 0.5, dot(named.astype(BF), earlier), -1.0)
    for h in range(4):
        meta_all[32 * h : 32 * h + 16, :] = slot[16 * h : 16 * h + 16].astype(BF)
        meta_all[32 * h + 16 : 32 * h + 32, :] = weight[16 * h : 16 * h + 16].astype(BF)
    row, col = iota((MAIN, MAIN), 0), iota((MAIN, MAIN), 1)
    perm[...] = jnp.where(col == (row & 15) * 16 + (row >> 4), 1.0, 0.0).astype(BF)
    expand[...] = jnp.where(iota((MAIN, NP), 0) >> 4 == iota((MAIN, NP), 1), 1.0, 0.0).astype(BF)

    pl.semaphore_wait(barrier, NP - 1 + 6)

    def along_z(c, a):
        remote(
            zl_ref.at[a, jnp.where(c == 3, 1, 0)], zl_ref.at[a, c],
            zs_sem.at[a, c - 1], zr_sem.at[a, c - 1], column(jnp.where(c == 1, -sign, 2 * sign)),
        ).start()

    loads[0].wait()
    along_z(1, 0)
    loads[1].wait()
    for j, offset in enumerate((-sign, 2 * sign, -3 * sign)):
        there = lax.div(lax.rem(z + offset + 2 * NZ, NZ), 2)
        remote(
            meta_all.at[pl.ds(pl.multiple_of(there * 32, 32), 32), :],
            meta.at[j + 1], ms_sem.at[j], mr_sem.at[j], column(offset),
        ).start()
    meta[0] = meta_all[pl.ds(pl.multiple_of(high * 32, 32), 32), :]

    def to_tiles(value):
        stacked = jnp.concatenate([value[:, LANE * j : LANE * (j + 1)] for j in range(16)], axis=0)
        return dot(perm[...], stacked).astype(BF)

    def from_tiles(tiles):
        stacked = dot(perm[...], tiles).astype(BF)
        return [stacked[16 * j : 16 * j + 16] for j in range(16)]

    def dispatch(c):
        @pl.when(c >= 1)
        def _():
            wait_for(meta.at[c], mr_sem.at[c - 1])

        slots, weights = meta[c, 0:16, :], meta[c, 16:32, :]
        at_slot = dot(expand[...], slots) == (iota((MAIN, T), 0) & 15).astype(F32)
        last = slots.astype(F32) == float(SLOTS)
        onehot[c, 0, 0:MAIN, :] = jnp.where(at_slot, 1.0, 0.0).astype(BF)
        onehot[c, 0, MAIN:ROWS, :] = jnp.where(last, 1.0, 0.0).astype(BF)
        onehot[c, 1, 0:MAIN, :] = jnp.where(at_slot, dot(expand[...], weights), 0.0).astype(BF)
        onehot[c, 1, MAIN:ROWS, :] = jnp.where(last, weights.astype(F32), 0.0).astype(BF)

        def one(a, carry):
            @pl.when(c >= 1)
            def _():
                wait_for(zl_ref.at[a, c], zr_sem.at[a, c - 1])

            @pl.when((c >= 1) & (2 * c + a < 7))
            def _():
                along_z(c + a, 1 - a)

            tail = []
            for r in range(4):
                packed = dot(onehot[c, a], zl_ref[a, c, :, QD * r : QD * (r + 1)]).astype(BF)
                snd[a, c, :, QD * r : QD * (r + 1)] = packed[0:MAIN]
                tail.append(packed[MAIN:ROWS])
            snd[a, c, :, D:WIDE] = to_tiles(jnp.concatenate(tail, axis=1))

            mine = pl.ds(pl.multiple_of(me * SLOTS, SLOTS), SLOTS)

            def send(step, carry):
                to = around(step)
                remote(
                    snd.at[a, c, pl.ds(pl.multiple_of(to * SLOTS, SLOTS), SLOTS), 0:WIDE],
                    rxz.at[a, c, mine, :], as_sem.at[a, c], ar_sem.at[a, c], plane(to),
                ).start()
                return carry

            lax.fori_loop(1, NP, send, 0)
            rxz[a, c, mine, :] = snd[a, c, mine, 0:WIDE]
            return carry

        lax.fori_loop(0, 2, one, 0)

    def expert(c):
        here = pl.ds(pl.multiple_of(c * MAIN, MAIN), MAIN)
        spare = pl.ds(pl.multiple_of(NCH * MAIN + c * NP, NP), NP)
        side = pl.ds(pl.multiple_of(c * NP, NP), NP)

        def arrive(a, rows):
            wait_for(rxz.at[a, c, 0:OTHERS, :], ar_sem.at[a, c])
            rows[0:MAIN, 0:D] = rxz[a, c, :, 0:D]
            for j, block in enumerate(from_tiles(rxz[a, c, :, D:WIDE])):
                rows[MAIN:ROWS, LANE * j : LANE * (j + 1)] = block
                extra[a, side, LANE * j : LANE * (j + 1)] = block

        arrive(0, rows_x)
        gate = dot(rows_x[:, 0:QD], wts[0, 0])
        up = dot(rows_x[:, 0:QD], wts[1, 0])
        for r in range(1, 4):
            part = slice(QD * r, QD * (r + 1))
            gate = gate + dot(rows_x[:, part], wts[0, r])
            up = up + dot(rows_x[:, part], wts[1, r])
        sig = jax.nn.sigmoid(gate)
        silu = gate * sig
        hidden = (silu * up).astype(BF)
        slope = up * sig * (1.0 + gate * (1.0 - sig))
        arrive(1, rows_z)
        back = dot(rows_z[:, 0:QD], wts[2, 0], 1, 1)
        for r in range(1, 4):
            back = back + dot(rows_z[:, QD * r : QD * (r + 1)], wts[2, r], 1, 1)
        prob = jnp.sum(hidden.astype(F32) * back, axis=1, keepdims=True)
        d_gate = (back * slope).astype(BF)
        d_up = (back * silu).astype(BF)
        for g, value in ((0, d_gate), (1, d_up), (2, hidden)):
            dall[g, here, :] = value[0:MAIN]
            dall[g, spare, :] = value[MAIN:ROWS]
        wait_for(snd.at[0, c, 0:OTHERS, 0:WIDE], as_sem.at[0, c])
        prob_main = jnp.broadcast_to(prob[0:MAIN], (MAIN, LANE))
        prob_last = dot(expand[...], jnp.broadcast_to(prob[MAIN:ROWS], (NP, LANE)).astype(BF))
        snd[0, c, :, WIDE:BACK] = jnp.where(
            iota((MAIN, LANE), 1) < 64, prob_main, prob_last
        ).astype(BF)

    def token_rows(c):
        here = pl.ds(pl.multiple_of(c * MAIN, MAIN), MAIN)
        spare = pl.ds(pl.multiple_of(NCH * MAIN + c * NP, NP), NP)
        d_gate, d_up = [jnp.concatenate([dall[g, here, :], dall[g, spare, :]]) for g in range(2)]
        tail = []
        for r in range(4):
            d_rows = (dot(d_gate, wts[0, r], 1, 1) + dot(d_up, wts[1, r], 1, 1)).astype(BF)
            snd[0, c, :, QD * r : QD * (r + 1)] = d_rows[0:MAIN]
            tail.append(d_rows[MAIN:ROWS])
        snd[0, c, :, D:WIDE] = to_tiles(jnp.concatenate(tail, axis=1))

    def give_back(c):
        mine = pl.ds(pl.multiple_of(me * SLOTS, SLOTS), SLOTS)

        def send(step, carry):
            to = around(step)
            remote(
                snd.at[0, c, pl.ds(pl.multiple_of(to * SLOTS, SLOTS), SLOTS), :],
                rrcv.at[c, mine, :], bs_sem.at[c], br_sem.at[c], plane(to),
            ).start()
            return carry

        lax.fori_loop(1, NP, send, 0)
        rrcv[c, mine, :] = snd[0, c, mine, :]

    def combine(c):
        wait_for(rrcv.at[c, 0:OTHERS, :], br_sem.at[c])
        rows_x[0:MAIN, 0:D] = rrcv[c, :, 0:D]
        for j, block in enumerate(from_tiles(rrcv[c, :, D:WIDE])):
            rows_x[MAIN:ROWS, LANE * j : LANE * (j + 1)] = block
        tile = rrcv[c, :, WIDE:BACK]
        of_slot = (onehot[c, 0, 0:MAIN, :].astype(F32) * tile[:, 0:1].astype(F32)).astype(BF)
        first = jnp.where(iota((NP, MAIN), 1) == iota((NP, MAIN), 0) * SLOTS, 1.0, 0.0).astype(BF)
        of_last = onehot[c, 0, MAIN:ROWS, :].astype(F32) * dot(first, tile)[:, 64:65]
        entries = dot(expand[...], of_slot, 0, 0) + of_last
        return dot(onehot[c, 0], rows_x[...], 0, 0), entries.astype(BF)

    def combine_far(c):
        rows, entries = combine(c)
        zsnd[c - 1] = rows.astype(BF)
        esnd[c - 1] = entries
        home = column(-c * sign)
        remote(zsnd.at[c - 1], zrcv.at[c - 1], ts_sem.at[c - 1], tr_sem.at[c - 1], home).start()
        remote(esnd.at[c - 1], ercv.at[c - 1], es_sem.at[c - 1], er_sem.at[c - 1], home).start()

    dispatch(0)
    for load in loads[2:]:
        load.wait()

    def step(c, carry):
        @pl.when(c < NCH - 1)
        def _():
            dispatch(c + 1)

        @pl.when(c == NCH - 2)
        def _():
            give_back(1)

        @pl.when(c == NCH - 1)
        def _():
            lax.fori_loop(0, 3, early_sums, 0)

        expert(c)

        @pl.when(c < NCH - 1)
        def _():
            token_rows(c)

        return carry

    old, old_tail = (NCH - 1) * MAIN, NCH * MAIN + (NCH - 1) * NP

    def width(r):
        return pl.ds(pl.multiple_of(r * QD, QD), QD)

    def early_sums(g, carry):
        a = lax.div(g, 2)
        for k, r in enumerate(((1 - low) * 2 + 1 - core, (1 - low) * 2 + core)):
            rows = rxz[a, 0 : NCH - 1, :, width(r)].reshape(old, QD)
            total = dot(dall[g, 0:old, :], rows, 0, 0)
            early[g, k] = total + dot(
                dall[g, NCH * MAIN : old_tail, :], extra[a, 0 : (NCH - 1) * NP, width(r)], 0, 0
            )
        return carry

    def whole_sum(g, k, r):
        a = lax.div(g, 2)
        total = early[g, k] + dot(
            dall[g, old : NCH * MAIN, :], rxz[a, NCH - 1, :, width(r)], 0, 0
        )
        return total + dot(
            dall[g, old_tail : NCH * ROWS, :], extra[a, (NCH - 1) * NP : NCH * NP, width(r)], 0, 0
        )

    def full_sum(g, r):
        a = lax.div(g, 2)
        rows = rxz[a, :, :, width(r)].reshape(NCH * MAIN, QD)
        total = dot(dall[g, 0 : NCH * MAIN, :], rows, 0, 0)
        return total + dot(dall[g, NCH * MAIN : NCH * ROWS, :], extra[a, :, width(r)], 0, 0)

    def to_core(g, half, total):
        gsum[g, half] = total.astype(BF)
        remote(
            gsum.at[g, half], core_rcv.at[g, half],
            cs_sem.at[g, half], cr_sem.at[g, half], other_core,
        ).start()

    def far_half(g, carry):
        to_core(g, 1 - low, whole_sum(g, 0, (1 - low) * 2 + 1 - core))
        return carry

    def to_low(g, carry):
        total = whole_sum(g, 1, (1 - low) * 2 + core)
        wait_for(core_rcv.at[g, 1 - low], cr_sem.at[g, 1 - low])
        lsnd[g] = (total + core_rcv[g, 1 - low].astype(F32)).astype(BF)
        remote(lsnd.at[g], low_rcv.at[g], ls_sem.at[g], lr_sem.at[g], other_low).start()
        return carry

    def near_half(g, carry):
        to_core(g, low, full_sum(g, low * 2 + 1 - core))
        return carry

    lax.fori_loop(0, NCH, step, 0)
    lax.fori_loop(0, 3, far_half, 0)
    lax.fori_loop(0, 3, to_low, 0)
    token_rows(NCH - 1)
    for c in (3, 2, 0):
        give_back(c)
    lax.fori_loop(0, 3, near_half, 0)
    combine_far(1)

    def to_own(g, carry):
        early[g, 0] = full_sum(g, low * 2 + core)
        return carry

    lax.fori_loop(0, 3, to_own, 0)
    combine_far(3)
    combine_far(2)
    rows, entries = combine(0)
    acc[...] = rows
    ent[pl.ds(pl.multiple_of(high * NP, NP), NP), :] = entries

    def finish(g):
        wait_for(core_rcv.at[g, low], cr_sem.at[g, low])
        wait_for(low_rcv.at[g], lr_sem.at[g])
        return early[g, 0] + core_rcv[g, low].astype(F32) + low_rcv[g].astype(F32)

    ggate_ref[...] = finish(0).T.astype(BF)
    gup_ref[...] = finish(1).T.astype(BF)
    gdown_ref[...] = finish(2).astype(BF)
    for j in range(NCH - 1):
        wait_for(zrcv.at[j], tr_sem.at[j])
    total = acc[...]
    for j in range(NCH - 1):
        total = total + zrcv[j].astype(F32)
    dtok_ref[...] = total.astype(BF)
    for j, offset in enumerate((-sign, 2 * sign, -3 * sign)):
        there = lax.div(lax.rem(z + offset + 2 * NZ, NZ), 2)
        wait_for(ercv.at[j], er_sem.at[j])
        ent[pl.ds(pl.multiple_of(there * NP, NP), NP), :] = ercv[j]
    entries = ent[...].astype(F32)
    d_probs = jnp.zeros((TOP, T), F32)
    for k in range(TOP):
        entry = jnp.sum(
            jnp.where(number == rank[k : k + 1, :], entries, 0.0), axis=0, keepdims=True
        )
        d_probs = d_probs + jnp.where(iota((TOP, T), 0) == k, entry, 0.0)
    dprob_ref[...] = (d_probs / probs).astype(BF)

    for j in range(NCH - 1):
        for a in range(2):
            wait_for(zl_ref.at[a, 0], zs_sem.at[a, j])
        wait_for(meta.at[0], ms_sem.at[j])
        wait_for(zsnd.at[j], ts_sem.at[j])
        wait_for(esnd.at[j], es_sem.at[j])
    for c in range(NCH):
        wait_for(snd.at[1, c, 0:OTHERS, 0:WIDE], as_sem.at[1, c])
        wait_for(snd.at[0, c, 0:OTHERS, :], bs_sem.at[c])
    for g in range(3):
        for half in range(2):
            wait_for(core_rcv.at[g, half], cs_sem.at[g, half])
        wait_for(low_rcv.at[g], ls_sem.at[g])


def shards(tokens, d_out, route_probs, routes, w_gate, w_up, w_down):
    dma = pltpu.SemaphoreType.DMA
    anywhere, vmem = pl.BlockSpec(memory_space=pl.ANY), pl.BlockSpec(memory_space=pltpu.VMEM)
    d_tokens, d_probs, g_gate, g_up, g_down = pl.pallas_call(
        kernel,
        out_shape=(
            jax.ShapeDtypeStruct((T, D), BF),
            jax.ShapeDtypeStruct((TOP, T), BF),
            jax.ShapeDtypeStruct((QD, F), BF),
            jax.ShapeDtypeStruct((QD, F), BF),
            jax.ShapeDtypeStruct((F, QD), BF),
        ),
        in_specs=[anywhere, anywhere, vmem, vmem, anywhere, anywhere, anywhere],
        out_specs=(vmem, vmem, vmem, vmem, vmem),
        scratch_shapes=[
            pltpu.VMEM((2, NCH, T, D), BF),
            pltpu.VMEM((T, LANE), BF),
            pltpu.VMEM((NCH, 32, LANE), BF),
            pltpu.VMEM((NCH, 2, ROWS, T), BF),
            pltpu.VMEM((MAIN, MAIN), BF),
            pltpu.VMEM((MAIN, NP), BF),
            pltpu.VMEM((2, NCH, MAIN, BACK), BF),
            pltpu.VMEM((2, NCH, MAIN, WIDE), BF),
            pltpu.VMEM((3, 4, F, QD), BF),
            pltpu.VMEM((ROWS, D), BF),
            pltpu.VMEM((ROWS, D), BF),
            pltpu.VMEM((2, NCH * NP, D), BF),
            pltpu.VMEM((3, NCH * ROWS, F), BF),
            pltpu.VMEM((NCH, MAIN, BACK), BF),
            pltpu.VMEM((NCH - 1, T, D), BF),
            pltpu.VMEM((NCH - 1, T, D), BF),
            pltpu.VMEM((NCH - 1, NP, T), BF),
            pltpu.VMEM((NCH - 1, NP, T), BF),
            pltpu.VMEM((4 * NP, T), BF),
            pltpu.VMEM((T, D), F32),
            pltpu.VMEM((3, 2, F, QD), F32),
            pltpu.VMEM((3, 2, F, QD), BF),
            pltpu.VMEM((3, F, QD), BF),
            pltpu.VMEM((3, 2, F, QD), BF),
            pltpu.VMEM((3, F, QD), BF),
            dma((8,)),
            dma((2, 3)), dma((2, 3)), dma((3,)), dma((3,)),
            dma((2, NCH)), dma((2, NCH)), dma((NCH,)), dma((NCH,)),
            dma((3,)), dma((3,)), dma((3,)), dma((3,)), dma((3, 2)), dma((3, 2)), dma((3,)), dma((3,)),
        ],
        compiler_params=pltpu.CompilerParams(
            collective_id=0, has_side_effects=True, vmem_limit_bytes=62 << 20
        ),
    )(
        tokens, d_out, route_probs.T, routes.T,
        w_gate.reshape(4, QD, F), w_up.reshape(4, QD, F), w_down.reshape(F, D),
    )
    return (
        d_tokens,
        d_probs.T,
        g_gate[None],
        g_up[None],
        g_down[None],
    )


def solution(mesh):
    return jax.shard_map(
        shards,
        mesh=mesh,
        in_specs=(
            P(("dp", "expert"), None),
            P(("dp", "expert"), None),
            P(("dp", "expert"), None),
            P(("dp", "expert"), None),
            P("expert", None, None),
            P("expert", None, None),
            P("expert", None, None),
        ),
        out_specs=(
            P(("dp", "expert"), None),
            P(("dp", "expert"), None),
            P("expert", "dp", None),
            P("expert", "dp", None),
            P("expert", None, "dp"),
        ),
        check_vma=False,
    )
```

```python
import jax
import jax.numpy as jnp
from jax import lax
from jax.experimental import pallas as pl
from jax.experimental.pallas import tpu as pltpu
from jax.sharding import PartitionSpec as P

MESH = pl.DeviceIdType.MESH
BF, F32 = jnp.bfloat16, jnp.float32

D = 2048
F = 512
T = 128
TOP = 8
NP = 16
NZ = 8
SLOTS = 16
MAIN = NP * SLOTS
ROWS = MAIN + NP
LANE = 128
WIDE = D + LANE
BACK = WIDE + LANE
NCH = 4
OTHERS = MAIN - SLOTS
QD = D // 4


def dot(left, right, left_dim=1, right_dim=0):
    return lax.dot_general(
        left, right, (((left_dim,), (right_dim,)), ((), ())), preferred_element_type=F32
    )


def iota(shape, dim):
    return lax.broadcasted_iota(jnp.int32, shape, dim)


def kernel(
    tok_hbm, dout_hbm, prob_ref, routes_ref, wg_hbm, wu_hbm, wd_hbm,
    dtok_ref, dprob_ref, grad_ref,
    zl_ref, meta_all, meta, onehot, perm, expand, snd, rxz, wts, rows_x, rows_z, extra,
    dall, rrcv, zsnd, zrcv, esnd, ercv, ent, acc, early, gsum, lsnd, core_rcv, low_rcv,
    load_sem, zs_sem, zr_sem, ms_sem, mr_sem, as_sem, ar_sem, bs_sem, br_sem,
    ts_sem, tr_sem, es_sem, er_sem, cs_sem, cr_sem, ls_sem, lr_sem,
):
    dp, ex = lax.axis_index("dp"), lax.axis_index("expert")
    core, low = lax.rem(dp, 2), lax.div(dp, 2)
    high, me = lax.rem(ex, 4), lax.div(ex, 4)
    z = high * 2 + low
    sign = 1 - 2 * low

    def column(offset):
        there = lax.rem(z + offset + 2 * NZ, NZ)
        return (lax.rem(there, 2) * 2 + core, me * 4 + lax.div(there, 2))

    def around(step):
        there_x = lax.rem(lax.div(me, 4) + lax.div(step, 4), 4)
        return there_x * 4 + lax.rem(lax.rem(me, 4) + lax.rem(step, 4), 4)

    def plane(number):
        return (dp, number * 4 + high)

    other_core = (low * 2 + 1 - core, ex)
    other_low = ((1 - low) * 2 + core, ex)

    def remote(src, dst, send, recv, device):
        return pltpu.make_async_remote_copy(
            src_ref=src, dst_ref=dst, send_sem=send, recv_sem=recv,
            device_id=device, device_id_type=MESH,
        )

    def wait_for(ref, sem):
        pltpu.make_async_copy(ref, ref, sem).wait()

    loads = [
        pltpu.make_async_copy(tok_hbm, zl_ref.at[0, 0], load_sem.at[0]),
        pltpu.make_async_copy(dout_hbm, zl_ref.at[1, 0], load_sem.at[1]),
        pltpu.make_async_copy(wg_hbm, wts.at[0], load_sem.at[2]),
        pltpu.make_async_copy(wu_hbm, wts.at[1], load_sem.at[3]),
    ] + [
        pltpu.make_async_copy(wd_hbm.at[:, QD * r : QD * (r + 1)], wts.at[2, r], load_sem.at[4 + r])
        for r in range(4)
    ]
    for load in loads:
        load.start()

    barrier = pltpu.get_barrier_semaphore()

    def greet(device):
        pl.semaphore_signal(barrier, inc=1, device_id=device, device_id_type=MESH)

    def greet_plane(step, carry):
        greet(plane(lax.rem(me + step, NP)))
        return carry

    lax.fori_loop(1, NP, greet_plane, 0)
    for offset in (-sign, -3 * sign, 2 * sign, -2 * sign):
        greet(column(offset))
    greet(other_core)
    greet(other_low)

    routes = routes_ref[...]
    rank = (routes & 3) * NP + (routes >> 2)
    probs = prob_ref[...].astype(F32)
    number = iota((64, T), 0)
    named = jnp.zeros((64, T), F32)
    weight = jnp.zeros((64, T), F32)
    for k in range(TOP):
        hit = rank[k : k + 1, :] == number
        named = named + jnp.where(hit, 1.0, 0.0)
        weight = weight + jnp.where(hit, probs[k : k + 1, :], 0.0)
    earlier = jnp.where(iota((T, T), 0) < iota((T, T), 1), 1.0, 0.0).astype(BF)
    slot = jnp.where(named > 0.5, dot(named.astype(BF), earlier), -1.0)
    for h in range(4):
        meta_all[32 * h : 32 * h + 16, :] = slot[16 * h : 16 * h + 16].astype(BF)
        meta_all[32 * h + 16 : 32 * h + 32, :] = weight[16 * h : 16 * h + 16].astype(BF)
    row, col = iota((MAIN, MAIN), 0), iota((MAIN, MAIN), 1)
    perm[...] = jnp.where(col == (row & 15) * 16 + (row >> 4), 1.0, 0.0).astype(BF)
    expand[...] = jnp.where(iota((MAIN, NP), 0) >> 4 == iota((MAIN, NP), 1), 1.0, 0.0).astype(BF)

    pl.semaphore_wait(barrier, NP - 1 + 6)

    def along_z(c, a):
        remote(
            zl_ref.at[a, jnp.where(c == 3, 1, 0)], zl_ref.at[a, c],
            zs_sem.at[a, c - 1], zr_sem.at[a, c - 1], column(jnp.where(c == 1, -sign, 2 * sign)),
        ).start()

    loads[0].wait()
    along_z(1, 0)
    loads[1].wait()
    for j, offset in enumerate((-sign, 2 * sign, -3 * sign)):
        there = lax.div(lax.rem(z + offset + 2 * NZ, NZ), 2)
        remote(
            meta_all.at[pl.ds(pl.multiple_of(there * 32, 32), 32), :],
            meta.at[j + 1], ms_sem.at[j], mr_sem.at[j], column(offset),
        ).start()
    meta[0] = meta_all[pl.ds(pl.multiple_of(high * 32, 32), 32), :]

    def to_tiles(value):
        stacked = jnp.concatenate([value[:, LANE * j : LANE * (j + 1)] for j in range(16)], axis=0)
        return dot(perm[...], stacked).astype(BF)

    def from_tiles(tiles):
        stacked = dot(perm[...], tiles).astype(BF)
        return [stacked[16 * j : 16 * j + 16] for j in range(16)]

    def dispatch(c):
        @pl.when(c >= 1)
        def _():
            wait_for(meta.at[c], mr_sem.at[c - 1])

        slots, weights = meta[c, 0:16, :], meta[c, 16:32, :]
        at_slot = dot(expand[...], slots) == (iota((MAIN, T), 0) & 15).astype(F32)
        last = slots.astype(F32) == float(SLOTS)
        onehot[c, 0, 0:MAIN, :] = jnp.where(at_slot, 1.0, 0.0).astype(BF)
        onehot[c, 0, MAIN:ROWS, :] = jnp.where(last, 1.0, 0.0).astype(BF)
        onehot[c, 1, 0:MAIN, :] = jnp.where(at_slot, dot(expand[...], weights), 0.0).astype(BF)
        onehot[c, 1, MAIN:ROWS, :] = jnp.where(last, weights.astype(F32), 0.0).astype(BF)

        def one(a, carry):
            @pl.when(c >= 1)
            def _():
                wait_for(zl_ref.at[a, c], zr_sem.at[a, c - 1])

            @pl.when((c >= 1) & (2 * c + a < 7))
            def _():
                along_z(c + a, 1 - a)

            tail = []
            for r in range(4):
                packed = dot(onehot[c, a], zl_ref[a, c, :, QD * r : QD * (r + 1)]).astype(BF)
                snd[a, c, :, QD * r : QD * (r + 1)] = packed[0:MAIN]
                tail.append(packed[MAIN:ROWS])
            snd[a, c, :, D:WIDE] = to_tiles(jnp.concatenate(tail, axis=1))

            mine = pl.ds(pl.multiple_of(me * SLOTS, SLOTS), SLOTS)

            def send(step, carry):
                to = around(step)
                remote(
                    snd.at[a, c, pl.ds(pl.multiple_of(to * SLOTS, SLOTS), SLOTS), 0:WIDE],
                    rxz.at[a, c, mine, :], as_sem.at[a, c], ar_sem.at[a, c], plane(to),
                ).start()
                return carry

            lax.fori_loop(1, NP, send, 0)
            rxz[a, c, mine, :] = snd[a, c, mine, 0:WIDE]
            return carry

        lax.fori_loop(0, 2, one, 0)

    def expert(c):
        here = pl.ds(pl.multiple_of(c * MAIN, MAIN), MAIN)
        spare = pl.ds(pl.multiple_of(NCH * MAIN + c * NP, NP), NP)
        side = pl.ds(pl.multiple_of(c * NP, NP), NP)

        def arrive(a, rows):
            wait_for(rxz.at[a, c, 0:OTHERS, :], ar_sem.at[a, c])
            rows[0:MAIN, 0:D] = rxz[a, c, :, 0:D]
            for j, block in enumerate(from_tiles(rxz[a, c, :, D:WIDE])):
                rows[MAIN:ROWS, LANE * j : LANE * (j + 1)] = block
                extra[a, side, LANE * j : LANE * (j + 1)] = block

        arrive(0, rows_x)
        gate = dot(rows_x[:, 0:QD], wts[0, 0])
        up = dot(rows_x[:, 0:QD], wts[1, 0])
        for r in range(1, 4):
            part = slice(QD * r, QD * (r + 1))
            gate = gate + dot(rows_x[:, part], wts[0, r])
            up = up + dot(rows_x[:, part], wts[1, r])
        sig = jax.nn.sigmoid(gate)
        silu = gate * sig
        hidden = (silu * up).astype(BF)
        slope = up * sig * (1.0 + gate * (1.0 - sig))
        arrive(1, rows_z)
        back = dot(rows_z[:, 0:QD], wts[2, 0], 1, 1)
        for r in range(1, 4):
            back = back + dot(rows_z[:, QD * r : QD * (r + 1)], wts[2, r], 1, 1)
        prob = jnp.sum(hidden.astype(F32) * back, axis=1, keepdims=True)
        d_gate = (back * slope).astype(BF)
        d_up = (back * silu).astype(BF)
        for g, value in ((0, d_gate), (1, d_up), (2, hidden)):
            dall[g, here, :] = value[0:MAIN]
            dall[g, spare, :] = value[MAIN:ROWS]
        wait_for(snd.at[0, c, 0:OTHERS, 0:WIDE], as_sem.at[0, c])
        prob_main = jnp.broadcast_to(prob[0:MAIN], (MAIN, LANE))
        prob_last = dot(expand[...], jnp.broadcast_to(prob[MAIN:ROWS], (NP, LANE)).astype(BF))
        snd[0, c, :, WIDE:BACK] = jnp.where(
            iota((MAIN, LANE), 1) < 64, prob_main, prob_last
        ).astype(BF)

    def token_rows(c):
        here = pl.ds(pl.multiple_of(c * MAIN, MAIN), MAIN)
        spare = pl.ds(pl.multiple_of(NCH * MAIN + c * NP, NP), NP)
        d_gate, d_up = [jnp.concatenate([dall[g, here, :], dall[g, spare, :]]) for g in range(2)]
        tail = []
        for r in range(4):
            d_rows = (dot(d_gate, wts[0, r], 1, 1) + dot(d_up, wts[1, r], 1, 1)).astype(BF)
            snd[0, c, :, QD * r : QD * (r + 1)] = d_rows[0:MAIN]
            tail.append(d_rows[MAIN:ROWS])
        snd[0, c, :, D:WIDE] = to_tiles(jnp.concatenate(tail, axis=1))

    def give_back(c):
        mine = pl.ds(pl.multiple_of(me * SLOTS, SLOTS), SLOTS)

        def send(step, carry):
            to = around(step)
            remote(
                snd.at[0, c, pl.ds(pl.multiple_of(to * SLOTS, SLOTS), SLOTS), :],
                rrcv.at[c, mine, :], bs_sem.at[c], br_sem.at[c], plane(to),
            ).start()
            return carry

        lax.fori_loop(1, NP, send, 0)
        rrcv[c, mine, :] = snd[0, c, mine, :]

    def combine(c):
        wait_for(rrcv.at[c, 0:OTHERS, :], br_sem.at[c])
        rows_x[0:MAIN, 0:D] = rrcv[c, :, 0:D]
        for j, block in enumerate(from_tiles(rrcv[c, :, D:WIDE])):
            rows_x[MAIN:ROWS, LANE * j : LANE * (j + 1)] = block
        tile = rrcv[c, :, WIDE:BACK]
        of_slot = (onehot[c, 0, 0:MAIN, :].astype(F32) * tile[:, 0:1].astype(F32)).astype(BF)
        first = jnp.where(iota((NP, MAIN), 1) == iota((NP, MAIN), 0) * SLOTS, 1.0, 0.0).astype(BF)
        of_last = onehot[c, 0, MAIN:ROWS, :].astype(F32) * dot(first, tile)[:, 64:65]
        entries = dot(expand[...], of_slot, 0, 0) + of_last
        return dot(onehot[c, 0], rows_x[...], 0, 0), entries.astype(BF)

    def combine_far(c):
        rows, entries = combine(c)
        zsnd[c - 1] = rows.astype(BF)
        esnd[c - 1] = entries
        home = column(-c * sign)
        remote(zsnd.at[c - 1], zrcv.at[c - 1], ts_sem.at[c - 1], tr_sem.at[c - 1], home).start()
        remote(esnd.at[c - 1], ercv.at[c - 1], es_sem.at[c - 1], er_sem.at[c - 1], home).start()

    dispatch(0)
    for load in loads[2:]:
        load.wait()

    def step(c, carry):
        @pl.when(c < NCH - 1)
        def _():
            dispatch(c + 1)

        @pl.when(c == NCH - 2)
        def _():
            give_back(1)

        @pl.when(c == NCH - 1)
        def _():
            lax.fori_loop(0, 3, early_sums, 0)

        expert(c)

        @pl.when(c < NCH - 1)
        def _():
            token_rows(c)

        return carry

    old, old_tail = (NCH - 1) * MAIN, NCH * MAIN + (NCH - 1) * NP

    def width(r):
        return pl.ds(pl.multiple_of(r * QD, QD), QD)

    def early_sums(g, carry):
        a = lax.div(g, 2)
        for k, r in enumerate(((1 - low) * 2 + 1 - core, (1 - low) * 2 + core)):
            rows = rxz[a, 0 : NCH - 1, :, width(r)].reshape(old, QD)
            total = dot(dall[g, 0:old, :], rows, 0, 0)
            early[g, k] = total + dot(
                dall[g, NCH * MAIN : old_tail, :], extra[a, 0 : (NCH - 1) * NP, width(r)], 0, 0
            )
        return carry

    def whole_sum(g, k, r):
        a = lax.div(g, 2)
        total = early[g, k] + dot(
            dall[g, old : NCH * MAIN, :], rxz[a, NCH - 1, :, width(r)], 0, 0
        )
        return total + dot(
            dall[g, old_tail : NCH * ROWS, :], extra[a, (NCH - 1) * NP : NCH * NP, width(r)], 0, 0
        )

    def full_sum(g, r):
        a = lax.div(g, 2)
        rows = rxz[a, :, :, width(r)].reshape(NCH * MAIN, QD)
        total = dot(dall[g, 0 : NCH * MAIN, :], rows, 0, 0)
        return total + dot(dall[g, NCH * MAIN : NCH * ROWS, :], extra[a, :, width(r)], 0, 0)

    def to_core(g, half, place, total):
        place[...] = total.astype(BF)
        remote(
            place, core_rcv.at[g, half],
            cs_sem.at[g, half], cr_sem.at[g, half], other_core,
        ).start()

    def far_half(g, carry):
        to_core(g, 1 - low, gsum.at[g], whole_sum(g, 0, (1 - low) * 2 + 1 - core))
        return carry

    def to_low(g, carry):
        total = whole_sum(g, 1, (1 - low) * 2 + core)
        wait_for(core_rcv.at[g, 1 - low], cr_sem.at[g, 1 - low])
        lsnd[g] = (total + core_rcv[g, 1 - low].astype(F32)).astype(BF)
        remote(lsnd.at[g], low_rcv.at[g], ls_sem.at[g], lr_sem.at[g], other_low).start()
        return carry

    def near_half(g, carry):
        to_core(g, low, wts.at[g, 0], full_sum(g, low * 2 + 1 - core))
        return carry

    lax.fori_loop(0, NCH, step, 0)
    lax.fori_loop(0, 3, far_half, 0)
    lax.fori_loop(0, 3, to_low, 0)
    token_rows(NCH - 1)
    for c in (3, 2, 0):
        give_back(c)
    lax.fori_loop(0, 3, near_half, 0)
    combine_far(1)

    def to_own(g, carry):
        early[g, 0] = full_sum(g, low * 2 + core)
        return carry

    lax.fori_loop(0, 3, to_own, 0)
    combine_far(3)
    combine_far(2)
    rows, entries = combine(0)
    wait_for(zrcv.at[0], tr_sem.at[0])
    acc[...] = rows + zrcv[0].astype(F32)
    ent[pl.ds(pl.multiple_of(high * NP, NP), NP), :] = entries

    def finish(g):
        wait_for(core_rcv.at[g, low], cr_sem.at[g, low])
        wait_for(low_rcv.at[g], lr_sem.at[g])
        return early[g, 0] + core_rcv[g, low].astype(F32) + low_rcv[g].astype(F32)

    grad_ref[0] = finish(0).T.astype(BF)
    grad_ref[1] = finish(1).T.astype(BF)
    grad_ref[2] = finish(2).astype(BF)
    for j in (2, 1):
        wait_for(zrcv.at[j], tr_sem.at[j])
    dtok_ref[...] = (acc[...] + zrcv[2].astype(F32) + zrcv[1].astype(F32)).astype(BF)
    for j, offset in enumerate((-sign, 2 * sign, -3 * sign)):
        there = lax.div(lax.rem(z + offset + 2 * NZ, NZ), 2)
        wait_for(ercv.at[j], er_sem.at[j])
        ent[pl.ds(pl.multiple_of(there * NP, NP), NP), :] = ercv[j]
    entries = ent[...].astype(F32)
    d_probs = jnp.zeros((TOP, T), F32)
    for k in range(TOP):
        entry = jnp.sum(
            jnp.where(number == rank[k : k + 1, :], entries, 0.0), axis=0, keepdims=True
        )
        d_probs = d_probs + jnp.where(iota((TOP, T), 0) == k, entry, 0.0)
    dprob_ref[...] = (d_probs / probs).astype(BF)

    for j in range(NCH - 1):
        for a in range(2):
            wait_for(zl_ref.at[a, 0], zs_sem.at[a, j])
        wait_for(meta.at[0], ms_sem.at[j])
        wait_for(zsnd.at[j], ts_sem.at[j])
        wait_for(esnd.at[j], es_sem.at[j])
    for c in range(NCH):
        wait_for(snd.at[1, c, 0:OTHERS, 0:WIDE], as_sem.at[1, c])
        wait_for(snd.at[0, c, 0:OTHERS, :], bs_sem.at[c])
    for g in range(3):
        for half in range(2):
            wait_for(core_rcv.at[g, half], cs_sem.at[g, half])
        wait_for(low_rcv.at[g], ls_sem.at[g])


def shards(tokens, d_out, route_probs, routes, w_gate, w_up, w_down):
    dma = pltpu.SemaphoreType.DMA
    anywhere, vmem = pl.BlockSpec(memory_space=pl.ANY), pl.BlockSpec(memory_space=pltpu.VMEM)
    d_tokens, d_probs, grads = pl.pallas_call(
        kernel,
        out_shape=(
            jax.ShapeDtypeStruct((T, D), BF),
            jax.ShapeDtypeStruct((TOP, T), BF),
            jax.ShapeDtypeStruct((3, F, QD), BF),
        ),
        in_specs=[anywhere, anywhere, vmem, vmem, anywhere, anywhere, anywhere],
        out_specs=(vmem, vmem, vmem),
        scratch_shapes=[
            pltpu.VMEM((2, NCH, T, D), BF),
            pltpu.VMEM((T, LANE), BF),
            pltpu.VMEM((NCH, 32, LANE), BF),
            pltpu.VMEM((NCH, 2, ROWS, T), BF),
            pltpu.VMEM((MAIN, MAIN), BF),
            pltpu.VMEM((MAIN, NP), BF),
            pltpu.VMEM((2, NCH, MAIN, BACK), BF),
            pltpu.VMEM((2, NCH, MAIN, WIDE), BF),
            pltpu.VMEM((3, 4, F, QD), BF),
            pltpu.VMEM((ROWS, D), BF),
            pltpu.VMEM((ROWS, D), BF),
            pltpu.VMEM((2, NCH * NP, D), BF),
            pltpu.VMEM((3, NCH * ROWS, F), BF),
            pltpu.VMEM((NCH, MAIN, BACK), BF),
            pltpu.VMEM((NCH - 1, T, D), BF),
            pltpu.VMEM((NCH - 1, T, D), BF),
            pltpu.VMEM((NCH - 1, NP, T), BF),
            pltpu.VMEM((NCH - 1, NP, T), BF),
            pltpu.VMEM((4 * NP, T), BF),
            pltpu.VMEM((T, D), F32),
            pltpu.VMEM((3, 2, F, QD), F32),
            pltpu.VMEM((3, F, QD), BF),
            pltpu.VMEM((3, F, QD), BF),
            pltpu.VMEM((3, 2, F, QD), BF),
            pltpu.VMEM((3, F, QD), BF),
            dma((8,)),
            dma((2, 3)), dma((2, 3)), dma((3,)), dma((3,)),
            dma((2, NCH)), dma((2, NCH)), dma((NCH,)), dma((NCH,)),
            dma((3,)), dma((3,)), dma((3,)), dma((3,)), dma((3, 2)), dma((3, 2)), dma((3,)), dma((3,)),
        ],
        compiler_params=pltpu.CompilerParams(
            collective_id=0, has_side_effects=True, vmem_limit_bytes=62 << 20
        ),
    )(
        tokens, d_out, route_probs.T, routes.T,
        w_gate.reshape(4, QD, F), w_up.reshape(4, QD, F), w_down.reshape(F, D),
    )
    return (
        d_tokens,
        d_probs.T,
        grads[0:1],
        grads[1:2],
        grads[2:3],
    )


def solution(mesh):
    return jax.shard_map(
        shards,
        mesh=mesh,
        in_specs=(
            P(("dp", "expert"), None),
            P(("dp", "expert"), None),
            P(("dp", "expert"), None),
            P(("dp", "expert"), None),
            P("expert", None, None),
            P("expert", None, None),
            P("expert", None, None),
        ),
        out_specs=(
            P(("dp", "expert"), None),
            P(("dp", "expert"), None),
            P("expert", "dp", None),
            P("expert", "dp", None),
            P("expert", None, "dp"),
        ),
        check_vma=False,
    )
```

```python
import jax
import jax.numpy as jnp
from jax import lax
from jax.experimental import pallas as pl
from jax.experimental.pallas import tpu as pltpu
from jax.sharding import PartitionSpec as P

MESH = pl.DeviceIdType.MESH
BF, F32 = jnp.bfloat16, jnp.float32

D = 2048
F = 512
T = 128
TOP = 8
NP = 16
NZ = 8
SLOTS = 16
MAIN = NP * SLOTS
ROWS = MAIN + NP
LANE = 128
WIDE = D + LANE
BACK = WIDE + LANE
NCH = 4
OTHERS = MAIN - SLOTS
QD = D // 4


def dot(left, right, left_dim=1, right_dim=0):
    return lax.dot_general(
        left, right, (((left_dim,), (right_dim,)), ((), ())), preferred_element_type=F32
    )


def iota(shape, dim):
    return lax.broadcasted_iota(jnp.int32, shape, dim)


def kernel(
    tok_hbm, dout_hbm, prob_ref, routes_ref, wg_hbm, wu_hbm, wd_hbm,
    dtok_ref, dprob_ref, grad_ref,
    zl_ref, meta_all, meta, onehot, perm, expand, snd, rxz, wts, rows_x, rows_z, extra,
    dall, rrcv, zsnd, zrcv, esnd, ercv, ent, acc, early, gsum, lsnd, core_rcv, low_rcv,
    load_sem, zs_sem, zr_sem, ms_sem, mr_sem, as_sem, ar_sem, bs_sem, br_sem,
    ts_sem, tr_sem, es_sem, er_sem, cs_sem, cr_sem, ls_sem, lr_sem,
):
    dp, ex = lax.axis_index("dp"), lax.axis_index("expert")
    core, low = lax.rem(dp, 2), lax.div(dp, 2)
    high, me = lax.rem(ex, 4), lax.div(ex, 4)
    z = high * 2 + low
    sign = 1 - 2 * low

    def column(offset):
        there = lax.rem(z + offset + 2 * NZ, NZ)
        return (lax.rem(there, 2) * 2 + core, me * 4 + lax.div(there, 2))

    def around(step):
        there_x = lax.rem(lax.div(me, 4) + lax.div(step, 4), 4)
        return there_x * 4 + lax.rem(lax.rem(me, 4) + lax.rem(step, 4), 4)

    def plane(number):
        return (dp, number * 4 + high)

    other_core = (low * 2 + 1 - core, ex)
    other_low = ((1 - low) * 2 + core, ex)

    def remote(src, dst, send, recv, device):
        return pltpu.make_async_remote_copy(
            src_ref=src, dst_ref=dst, send_sem=send, recv_sem=recv,
            device_id=device, device_id_type=MESH,
        )

    def wait_for(ref, sem):
        pltpu.make_async_copy(ref, ref, sem).wait()

    loads = [
        pltpu.make_async_copy(tok_hbm, zl_ref.at[0, 0], load_sem.at[0]),
        pltpu.make_async_copy(dout_hbm, zl_ref.at[1, 0], load_sem.at[1]),
        pltpu.make_async_copy(wg_hbm, wts.at[0], load_sem.at[2]),
        pltpu.make_async_copy(wu_hbm, wts.at[1], load_sem.at[3]),
    ] + [
        pltpu.make_async_copy(wd_hbm.at[:, QD * r : QD * (r + 1)], wts.at[2, r], load_sem.at[4 + r])
        for r in range(4)
    ]
    for load in loads:
        load.start()

    barrier = pltpu.get_barrier_semaphore()

    def greet(device):
        pl.semaphore_signal(barrier, inc=1, device_id=device, device_id_type=MESH)

    def greet_plane(step, carry):
        greet(plane(lax.rem(me + step, NP)))
        return carry

    lax.fori_loop(1, NP, greet_plane, 0)
    for offset in (-sign, -3 * sign, 2 * sign, -2 * sign):
        greet(column(offset))
    greet(other_core)
    greet(other_low)

    routes = routes_ref[...]
    rank = (routes & 3) * NP + (routes >> 2)
    probs = prob_ref[...].astype(F32)
    number = iota((64, T), 0)
    named = jnp.zeros((64, T), F32)
    weight = jnp.zeros((64, T), F32)
    for k in range(TOP):
        hit = rank[k : k + 1, :] == number
        named = named + jnp.where(hit, 1.0, 0.0)
        weight = weight + jnp.where(hit, probs[k : k + 1, :], 0.0)
    earlier = jnp.where(iota((T, T), 0) < iota((T, T), 1), 1.0, 0.0).astype(BF)
    slot = jnp.where(named > 0.5, dot(named.astype(BF), earlier), -1.0)
    for h in range(4):
        meta_all[32 * h : 32 * h + 16, :] = slot[16 * h : 16 * h + 16].astype(BF)
        meta_all[32 * h + 16 : 32 * h + 32, :] = weight[16 * h : 16 * h + 16].astype(BF)
    row, col = iota((MAIN, MAIN), 0), iota((MAIN, MAIN), 1)
    perm[...] = jnp.where(col == (row & 15) * 16 + (row >> 4), 1.0, 0.0).astype(BF)
    expand[...] = jnp.where(iota((MAIN, NP), 0) >> 4 == iota((MAIN, NP), 1), 1.0, 0.0).astype(BF)

    pl.semaphore_wait(barrier, NP - 1 + 6)

    def along_z(c, a):
        remote(
            zl_ref.at[a, jnp.where(c == 3, 1, 0)], zl_ref.at[a, c],
            zs_sem.at[a, c - 1], zr_sem.at[a, c - 1], column(jnp.where(c == 1, -sign, 2 * sign)),
        ).start()

    loads[0].wait()
    along_z(1, 0)
    loads[1].wait()
    for j, offset in enumerate((-sign, 2 * sign, -3 * sign)):
        there = lax.div(lax.rem(z + offset + 2 * NZ, NZ), 2)
        remote(
            meta_all.at[pl.ds(pl.multiple_of(there * 32, 32), 32), :],
            meta.at[j + 1], ms_sem.at[j], mr_sem.at[j], column(offset),
        ).start()
    meta[0] = meta_all[pl.ds(pl.multiple_of(high * 32, 32), 32), :]

    def to_tiles(value):
        stacked = jnp.concatenate([value[:, LANE * j : LANE * (j + 1)] for j in range(16)], axis=0)
        return dot(perm[...], stacked).astype(BF)

    def from_tiles(tiles):
        stacked = dot(perm[...], tiles).astype(BF)
        return [stacked[16 * j : 16 * j + 16] for j in range(16)]

    def dispatch(c):
        @pl.when(c >= 1)
        def _():
            wait_for(meta.at[c], mr_sem.at[c - 1])

        slots, weights = meta[c, 0:16, :], meta[c, 16:32, :]
        at_slot = dot(expand[...], slots) == (iota((MAIN, T), 0) & 15).astype(F32)
        last = slots.astype(F32) == float(SLOTS)
        onehot[c, 0, 0:MAIN, :] = jnp.where(at_slot, 1.0, 0.0).astype(BF)
        onehot[c, 0, MAIN:ROWS, :] = jnp.where(last, 1.0, 0.0).astype(BF)
        onehot[c, 1, 0:MAIN, :] = jnp.where(at_slot, dot(expand[...], weights), 0.0).astype(BF)
        onehot[c, 1, MAIN:ROWS, :] = jnp.where(last, weights.astype(F32), 0.0).astype(BF)

        def one(a, carry):
            @pl.when(c >= 1)
            def _():
                wait_for(zl_ref.at[a, c], zr_sem.at[a, c - 1])

            @pl.when((c >= 1) & (2 * c + a < 7))
            def _():
                along_z(c + a, 1 - a)

            tail = []
            for r in range(4):
                packed = dot(onehot[c, a], zl_ref[a, c, :, QD * r : QD * (r + 1)]).astype(BF)
                snd[a, c, :, QD * r : QD * (r + 1)] = packed[0:MAIN]
                tail.append(packed[MAIN:ROWS])
            snd[a, c, :, D:WIDE] = to_tiles(jnp.concatenate(tail, axis=1))

            mine = pl.ds(pl.multiple_of(me * SLOTS, SLOTS), SLOTS)

            def send(step, carry):
                to = around(step)
                remote(
                    snd.at[a, c, pl.ds(pl.multiple_of(to * SLOTS, SLOTS), SLOTS), 0:WIDE],
                    rxz.at[a, c, mine, :], as_sem.at[a, c], ar_sem.at[a, c], plane(to),
                ).start()
                return carry

            lax.fori_loop(1, NP, send, 0)
            rxz[a, c, mine, :] = snd[a, c, mine, 0:WIDE]
            return carry

        lax.fori_loop(0, 2, one, 0)

    def expert(c):
        here = pl.ds(pl.multiple_of(c * MAIN, MAIN), MAIN)
        spare = pl.ds(pl.multiple_of(NCH * MAIN + c * NP, NP), NP)
        side = pl.ds(pl.multiple_of(c * NP, NP), NP)

        def arrive(a, rows):
            wait_for(rxz.at[a, c, 0:OTHERS, :], ar_sem.at[a, c])
            rows[0:MAIN, 0:D] = rxz[a, c, :, 0:D]
            for j, block in enumerate(from_tiles(rxz[a, c, :, D:WIDE])):
                rows[MAIN:ROWS, LANE * j : LANE * (j + 1)] = block
                extra[a, side, LANE * j : LANE * (j + 1)] = block

        arrive(0, rows_x)
        gate = dot(rows_x[:, 0:QD], wts[0, 0])
        up = dot(rows_x[:, 0:QD], wts[1, 0])
        for r in range(1, 4):
            part = slice(QD * r, QD * (r + 1))
            gate = gate + dot(rows_x[:, part], wts[0, r])
            up = up + dot(rows_x[:, part], wts[1, r])
        sig = jax.nn.sigmoid(gate)
        silu = gate * sig
        hidden = (silu * up).astype(BF)
        slope = up * sig * (1.0 + gate * (1.0 - sig))
        arrive(1, rows_z)
        back = dot(rows_z[:, 0:QD], wts[2, 0], 1, 1)
        for r in range(1, 4):
            back = back + dot(rows_z[:, QD * r : QD * (r + 1)], wts[2, r], 1, 1)
        prob = jnp.sum(hidden.astype(F32) * back, axis=1, keepdims=True)
        d_gate = (back * slope).astype(BF)
        d_up = (back * silu).astype(BF)
        for g, value in ((0, d_gate), (1, d_up), (2, hidden)):
            dall[g, here, :] = value[0:MAIN]
            dall[g, spare, :] = value[MAIN:ROWS]
        wait_for(snd.at[0, c, 0:OTHERS, 0:WIDE], as_sem.at[0, c])
        prob_main = jnp.broadcast_to(prob[0:MAIN], (MAIN, LANE))
        prob_last = dot(expand[...], jnp.broadcast_to(prob[MAIN:ROWS], (NP, LANE)).astype(BF))
        snd[0, c, :, WIDE:BACK] = jnp.where(
            iota((MAIN, LANE), 1) < 64, prob_main, prob_last
        ).astype(BF)

    def token_rows(c):
        here = pl.ds(pl.multiple_of(c * MAIN, MAIN), MAIN)
        spare = pl.ds(pl.multiple_of(NCH * MAIN + c * NP, NP), NP)
        d_gate, d_up = [jnp.concatenate([dall[g, here, :], dall[g, spare, :]]) for g in range(2)]
        tail = []
        for r in range(4):
            d_rows = (dot(d_gate, wts[0, r], 1, 1) + dot(d_up, wts[1, r], 1, 1)).astype(BF)
            snd[0, c, :, QD * r : QD * (r + 1)] = d_rows[0:MAIN]
            tail.append(d_rows[MAIN:ROWS])
        snd[0, c, :, D:WIDE] = to_tiles(jnp.concatenate(tail, axis=1))

    def give_back(c):
        mine = pl.ds(pl.multiple_of(me * SLOTS, SLOTS), SLOTS)

        def send(step, carry):
            to = around(step)
            remote(
                snd.at[0, c, pl.ds(pl.multiple_of(to * SLOTS, SLOTS), SLOTS), :],
                rrcv.at[c, mine, :], bs_sem.at[c], br_sem.at[c], plane(to),
            ).start()
            return carry

        lax.fori_loop(1, NP, send, 0)
        rrcv[c, mine, :] = snd[0, c, mine, :]

    def combine(c):
        wait_for(rrcv.at[c, 0:OTHERS, :], br_sem.at[c])
        rows_x[0:MAIN, 0:D] = rrcv[c, :, 0:D]
        for j, block in enumerate(from_tiles(rrcv[c, :, D:WIDE])):
            rows_x[MAIN:ROWS, LANE * j : LANE * (j + 1)] = block
        tile = rrcv[c, :, WIDE:BACK]
        of_slot = (onehot[c, 0, 0:MAIN, :].astype(F32) * tile[:, 0:1].astype(F32)).astype(BF)
        first = jnp.where(iota((NP, MAIN), 1) == iota((NP, MAIN), 0) * SLOTS, 1.0, 0.0).astype(BF)
        of_last = onehot[c, 0, MAIN:ROWS, :].astype(F32) * dot(first, tile)[:, 64:65]
        entries = dot(expand[...], of_slot, 0, 0) + of_last
        return dot(onehot[c, 0], rows_x[...], 0, 0), entries.astype(BF)

    def combine_far(c):
        rows, entries = combine(c)
        zsnd[c - 1] = rows.astype(BF)
        esnd[c - 1] = entries
        home = column(-c * sign)
        remote(zsnd.at[c - 1], zrcv.at[c - 1], ts_sem.at[c - 1], tr_sem.at[c - 1], home).start()
        remote(esnd.at[c - 1], ercv.at[c - 1], es_sem.at[c - 1], er_sem.at[c - 1], home).start()

    dispatch(0)
    for load in loads[2:]:
        load.wait()

    def step(c, carry):
        @pl.when(c < NCH - 1)
        def _():
            dispatch(c + 1)

        @pl.when(c == NCH - 2)
        def _():
            give_back(1)

        @pl.when(c == NCH - 1)
        def _():
            lax.fori_loop(0, 3, early_sums, 0)

        expert(c)

        @pl.when(c < NCH - 1)
        def _():
            token_rows(c)

        return carry

    old, old_tail = (NCH - 1) * MAIN, NCH * MAIN + (NCH - 1) * NP

    def width(r):
        return pl.ds(pl.multiple_of(r * QD, QD), QD)

    def early_sums(g, carry):
        a = lax.div(g, 2)
        for k, r in enumerate(((1 - low) * 2 + 1 - core, (1 - low) * 2 + core)):
            rows = rxz[a, 0 : NCH - 1, :, width(r)].reshape(old, QD)
            total = dot(dall[g, 0:old, :], rows, 0, 0)
            early[g, k] = total + dot(
                dall[g, NCH * MAIN : old_tail, :], extra[a, 0 : (NCH - 1) * NP, width(r)], 0, 0
            )
        return carry

    def whole_sum(g, k, r):
        a = lax.div(g, 2)
        total = early[g, k] + dot(
            dall[g, old : NCH * MAIN, :], rxz[a, NCH - 1, :, width(r)], 0, 0
        )
        return total + dot(
            dall[g, old_tail : NCH * ROWS, :], extra[a, (NCH - 1) * NP : NCH * NP, width(r)], 0, 0
        )

    def full_sum(g, r):
        a = lax.div(g, 2)
        rows = rxz[a, :, :, width(r)].reshape(NCH * MAIN, QD)
        total = dot(dall[g, 0 : NCH * MAIN, :], rows, 0, 0)
        return total + dot(dall[g, NCH * MAIN : NCH * ROWS, :], extra[a, :, width(r)], 0, 0)

    def to_core(g, half, place, total):
        place[...] = total.astype(BF)
        remote(
            place, core_rcv.at[g, half],
            cs_sem.at[g, half], cr_sem.at[g, half], other_core,
        ).start()

    def far_half(g, carry):
        to_core(g, 1 - low, gsum.at[g], whole_sum(g, 0, (1 - low) * 2 + 1 - core))
        return carry

    def to_low(g, carry):
        total = whole_sum(g, 1, (1 - low) * 2 + core)
        wait_for(core_rcv.at[g, 1 - low], cr_sem.at[g, 1 - low])
        lsnd[g] = (total + core_rcv[g, 1 - low].astype(F32)).astype(BF)
        remote(lsnd.at[g], low_rcv.at[g], ls_sem.at[g], lr_sem.at[g], other_low).start()
        return carry

    def near_half(g, carry):
        to_core(g, low, wts.at[g, 0], full_sum(g, low * 2 + 1 - core))
        return carry

    lax.fori_loop(0, NCH, step, 0)
    def far_then_low(g, carry):
        @pl.when(g < 3)
        def _():
            far_half(g, 0)

        @pl.when(g >= 1)
        def _():
            to_low(g - 1, 0)

        return carry

    lax.fori_loop(0, 2, far_then_low, 0)
    token_rows(NCH - 1)
    give_back(3)
    lax.fori_loop(2, 4, far_then_low, 0)
    combine_far(1)
    for c in (2, 0):
        give_back(c)
    lax.fori_loop(0, 3, near_half, 0)

    def to_own(g, carry):
        early[g, 0] = full_sum(g, low * 2 + core)
        return carry

    combine_far(3)
    lax.fori_loop(0, 3, to_own, 0)
    combine_far(2)
    rows, entries = combine(0)
    wait_for(zrcv.at[0], tr_sem.at[0])
    acc[...] = rows + zrcv[0].astype(F32)
    ent[pl.ds(pl.multiple_of(high * NP, NP), NP), :] = entries

    def finish(g):
        wait_for(core_rcv.at[g, low], cr_sem.at[g, low])
        wait_for(low_rcv.at[g], lr_sem.at[g])
        return early[g, 0] + core_rcv[g, low].astype(F32) + low_rcv[g].astype(F32)

    grad_ref[0] = finish(0).T.astype(BF)
    grad_ref[1] = finish(1).T.astype(BF)
    grad_ref[2] = finish(2).astype(BF)
    for j in (2, 1):
        wait_for(zrcv.at[j], tr_sem.at[j])
    dtok_ref[...] = (acc[...] + zrcv[2].astype(F32) + zrcv[1].astype(F32)).astype(BF)
    for j, offset in enumerate((-sign, 2 * sign, -3 * sign)):
        there = lax.div(lax.rem(z + offset + 2 * NZ, NZ), 2)
        wait_for(ercv.at[j], er_sem.at[j])
        ent[pl.ds(pl.multiple_of(there * NP, NP), NP), :] = ercv[j]
    entries = ent[...].astype(F32)
    d_probs = jnp.zeros((TOP, T), F32)
    for k in range(TOP):
        entry = jnp.sum(
            jnp.where(number == rank[k : k + 1, :], entries, 0.0), axis=0, keepdims=True
        )
        d_probs = d_probs + jnp.where(iota((TOP, T), 0) == k, entry, 0.0)
    dprob_ref[...] = (d_probs / probs).astype(BF)

    for j in range(NCH - 1):
        for a in range(2):
            wait_for(zl_ref.at[a, 0], zs_sem.at[a, j])
        wait_for(meta.at[0], ms_sem.at[j])
        wait_for(zsnd.at[j], ts_sem.at[j])
        wait_for(esnd.at[j], es_sem.at[j])
    for c in range(NCH):
        wait_for(snd.at[1, c, 0:OTHERS, 0:WIDE], as_sem.at[1, c])
        wait_for(snd.at[0, c, 0:OTHERS, :], bs_sem.at[c])
    for g in range(3):
        for half in range(2):
            wait_for(core_rcv.at[g, half], cs_sem.at[g, half])
        wait_for(low_rcv.at[g], ls_sem.at[g])


def shards(tokens, d_out, route_probs, routes, w_gate, w_up, w_down):
    dma = pltpu.SemaphoreType.DMA
    anywhere, vmem = pl.BlockSpec(memory_space=pl.ANY), pl.BlockSpec(memory_space=pltpu.VMEM)
    d_tokens, d_probs, grads = pl.pallas_call(
        kernel,
        out_shape=(
            jax.ShapeDtypeStruct((T, D), BF),
            jax.ShapeDtypeStruct((TOP, T), BF),
            jax.ShapeDtypeStruct((3, F, QD), BF),
        ),
        in_specs=[anywhere, anywhere, vmem, vmem, anywhere, anywhere, anywhere],
        out_specs=(vmem, vmem, vmem),
        scratch_shapes=[
            pltpu.VMEM((2, NCH, T, D), BF),
            pltpu.VMEM((T, LANE), BF),
            pltpu.VMEM((NCH, 32, LANE), BF),
            pltpu.VMEM((NCH, 2, ROWS, T), BF),
            pltpu.VMEM((MAIN, MAIN), BF),
            pltpu.VMEM((MAIN, NP), BF),
            pltpu.VMEM((2, NCH, MAIN, BACK), BF),
            pltpu.VMEM((2, NCH, MAIN, WIDE), BF),
            pltpu.VMEM((3, 4, F, QD), BF),
            pltpu.VMEM((ROWS, D), BF),
            pltpu.VMEM((ROWS, D), BF),
            pltpu.VMEM((2, NCH * NP, D), BF),
            pltpu.VMEM((3, NCH * ROWS, F), BF),
            pltpu.VMEM((NCH, MAIN, BACK), BF),
            pltpu.VMEM((NCH - 1, T, D), BF),
            pltpu.VMEM((NCH - 1, T, D), BF),
            pltpu.VMEM((NCH - 1, NP, T), BF),
            pltpu.VMEM((NCH - 1, NP, T), BF),
            pltpu.VMEM((4 * NP, T), BF),
            pltpu.VMEM((T, D), F32),
            pltpu.VMEM((3, 2, F, QD), F32),
            pltpu.VMEM((3, F, QD), BF),
            pltpu.VMEM((3, F, QD), BF),
            pltpu.VMEM((3, 2, F, QD), BF),
            pltpu.VMEM((3, F, QD), BF),
            dma((8,)),
            dma((2, 3)), dma((2, 3)), dma((3,)), dma((3,)),
            dma((2, NCH)), dma((2, NCH)), dma((NCH,)), dma((NCH,)),
            dma((3,)), dma((3,)), dma((3,)), dma((3,)), dma((3, 2)), dma((3, 2)), dma((3,)), dma((3,)),
        ],
        compiler_params=pltpu.CompilerParams(
            collective_id=0, has_side_effects=True, vmem_limit_bytes=62 << 20
        ),
    )(
        tokens, d_out, route_probs.T, routes.T,
        w_gate.reshape(4, QD, F), w_up.reshape(4, QD, F), w_down.reshape(F, D),
    )
    return (
        d_tokens,
        d_probs.T,
        grads[0:1],
        grads[1:2],
        grads[2:3],
    )


def solution(mesh):
    return jax.shard_map(
        shards,
        mesh=mesh,
        in_specs=(
            P(("dp", "expert"), None),
            P(("dp", "expert"), None),
            P(("dp", "expert"), None),
            P(("dp", "expert"), None),
            P("expert", None, None),
            P("expert", None, None),
            P("expert", None, None),
        ),
        out_specs=(
            P(("dp", "expert"), None),
            P(("dp", "expert"), None),
            P("expert", "dp", None),
            P("expert", "dp", None),
            P("expert", None, "dp"),
        ),
        check_vma=False,
    )
```
